128 devices in a mesh: band: 32 (over z, x, core), tile: 4 (over y).
Axes of the slice: x: 4, y: 4, z: 4, core: 2. Of those that a mesh axis runs over, the one named last changes fastest.
Arguments:
- source: bfloat16 [40, 1048576], P(None, ('band', 'tile')), may hold values from -6 to 6
- regrid_weights: bfloat16 [8192, 4, 128, 128], P(('band', 'tile')), may hold values from -0.5 to 0.5
- dest_group: int32 [8192, 4], P(('band', 'tile')), may hold values from 0 to 127, all different within a row; in each aligned block of 64 rows (0 to 63, 64 to 127, ...) at most 6 rows name the same one
- dest_block: int32 [8192, 4], P(('band', 'tile')), may hold values from 0 to 191
- seam_table: int32 [12, 4, 3], replicated, may hold values from 0 to 11, as said below
- conv1_weight: bfloat16 [9, 128, 40], replicated, may hold values from -0.3125 to 0.3125
- conv1_bias: float32 [128], replicated, may hold values from -3 to 3
- conv2_weight: bfloat16 [9, 128, 128], replicated, may hold values from -0.1875 to 0.1875
- conv2_bias: float32 [128], replicated, may hold values from -3 to 3
Outputs:
- features: bfloat16 [128, 12, 512, 512], P(None, None, 'band', 'tile')
The draws below stay inside these ranges and needn't reach their ends.
Inputs may be any that keep to these rules, and one draw needn't show every extreme that they name: `dest_group`: within the rows of one device (aligned blocks of 64 rows) no value appears more than 6 times, and a row's 4 values differ. `seam_table`: entries 0 and 1 name a face and a side (0 to 3). Joins are symmetric: if side s of face f is joined to side s2 of face g, side s2 of face g is joined to side s of face f with the same reversal entry. No side is joined to itself. Entry 2 is 0 or 1.
All inputs are finite; a program needn't handle non-finite values.
Results may differ from the reference program's by a relative error of at most 0.0058.
Values may be sent and summed in bfloat16 or wider, within the bound.
No kernel may reach another device: no remote copies, remote signals or barrier semaphores. Data moves between devices by JAX's collectives and lax.ppermute only.
A program may use at most 320 MiB of HBM per device.

```python
import math
import jax
import jax.numpy as jnp
import numpy as np
from jax import lax

FIELDS = 40
HID = 128
BLK = 128
FACES = 12
KB = 4
SB_DEV = 64
C = 6
NSIDE = 512
ROWS_DEV = 16
TB_DEV = 192
SRC_BLOCKS = 8192
SRC_CELLS = 1048576
N_BAND = 32
N_TILE = 4
DEVICES = 128


def draw_seam_table(key, part):
    order = jax.random.permutation(key, 4 * FACES).astype(jnp.int32)
    firsts = order[0::2]
    seconds = order[1::2]
    partner = jnp.zeros((4 * FACES,), jnp.int32).at[firsts].set(seconds).at[seconds].set(firsts)
    flips = jax.random.randint(jax.random.fold_in(key, 7), (2 * FACES,), 0, 2).astype(jnp.int32)
    reverse = jnp.zeros((4 * FACES,), jnp.int32).at[firsts].set(flips).at[seconds].set(flips)
    return jnp.stack((partner // 4, partner % 4, reverse), axis=1).reshape(FACES, 4, 3).astype(jnp.int32)


def with_ends(values, own_key, low, high):
    extent = values.shape
    place = [jax.random.randint(jax.random.fold_in(own_key, axis), (), 0, extent[axis]) for axis in range(len(extent))]
    values = values.at[tuple(place)].set(low)
    longest = extent.index(max(extent))
    place[longest] = (place[longest] + 1) % extent[longest]
    return values.at[tuple(place)].set(high)


def block_scale(own_key, extent, pieces, smallest, largest):
    loudness = 1.0
    for position, shards_of in pieces:
        heights = jax.random.uniform(jax.random.fold_in(jax.random.fold_in(own_key, 6), position), (shards_of,), jnp.float32, smallest / len(pieces), largest / len(pieces))
        loudness = loudness * jnp.repeat(jnp.exp(heights), extent[position] // shards_of).reshape((-1,) + (1,) * (len(extent) - 1 - position))
    return loudness


def routed_block(rng, own, number, rows, number_of, top, limit, lean):
    sequence = jax.random.permutation(rng, number_of)
    heavy_load, common = portions_of(number_of, rows * top, limit, lean, True), portions_of(number_of, rows * top, limit, lean, False)
    places = jnp.arange(number_of)

    def named(sizes, turn):
        used = int((sizes > 0).sum())
        fixed = max(1, used // 4)
        shifted = fixed + (places - fixed + turn * (used - fixed)) % max(1, number_of - fixed)
        return jnp.zeros((number_of,), jnp.int32).at[sequence[jnp.where(places < fixed, places, shifted)]].set(jnp.asarray(sizes, jnp.int32))

    sizes = jnp.where(number % 4 == 0, named(heavy_load, number // 4), named(common, number - number // 4 - 1))
    mixed = jax.random.permutation(jax.random.fold_in(own, 3), number_of)
    source_of, taker = mixed[0:number_of // 2 * 2:2], mixed[1:number_of // 2 * 2:2]
    room = jnp.minimum(sizes[source_of] - 1, limit - sizes[taker]) // 2
    room = jnp.where((source_of == sequence[0]) | (taker == sequence[0]) | (sizes[taker] == 0), 0, jnp.maximum(room, 0))
    shifted = jax.random.randint(jax.random.fold_in(own, 4), (number_of // 2,), 0, 1 << 20) % (room + 1)
    sizes = sizes.at[source_of].add(-shifted).at[taker].add(shifted)
    items = jnp.searchsorted(jnp.cumsum(sizes), jnp.arange(rows * top), side="right").astype(jnp.int32)
    listing = items.reshape(top, rows).T
    listing = listing[jax.random.permutation(jax.random.fold_in(own, 1), rows)]
    turn = jax.random.randint(jax.random.fold_in(own, 2), (rows, 1), 0, top)
    return jnp.take_along_axis(listing, (jnp.arange(top)[None, :] + turn) % top, axis=1)


def portions_of(amount, total, limit, slope, full):
    portions = [(1 << 20) // math.isqrt(rank ** slope) + 1 for rank in range(1, amount + 1)]
    largest = limit if full else min(limit, max(-(-total // amount), total * portions[0] // sum(portions)))
    least = 1 if total - largest >= amount - 1 else 0
    holding, spare = [largest] + [least] * (amount - 1), total - largest - least * (amount - 1)
    while spare > 0:
        candidates = [i for i in range(1, amount) if holding[i] < largest] or [i for i in range(1, amount) if holding[i] < limit]
        pool, remaining = sum([portions[i] for i in candidates]), spare
        for i in candidates:
            addition = min(limit - holding[i], max(1, remaining * portions[i] // pool), spare)
            holding[i] = holding[i] + addition
            spare = spare - addition
    return np.array(holding)


def noise(rng, dims, scale, reach, pieces=(), held_as=jnp.bfloat16):
    entries = jax.random.normal(rng, dims, jnp.float32) * scale
    if len(pieces) > 0:
        entries = block_scale(rng, dims, pieces, -0.22, 0.18) * entries
    return jnp.clip(entries, min=-reach, max=reach).astype(held_as)


def setup_inputs(seed: int = 0) -> dict:
    seeds = jax.random.split(jax.random.key(seed), 10)
    source = noise(seeds[0], (FIELDS, SRC_CELLS), 1.0, 6.0, ((1, 128),))
    regrid_weights = noise(seeds[1], (SRC_BLOCKS, KB, BLK, BLK), BLK ** -0.5, 0.5, ((0, 128),))
    dest_group_keys = jax.random.split(jax.random.fold_in(seeds[2], 1), SRC_BLOCKS // SB_DEV)
    dest_group_turns = jax.random.permutation(jax.random.fold_in(seeds[2], 3), SRC_BLOCKS // SB_DEV)
    dest_group = jax.vmap(lambda own, number: routed_block(jax.random.fold_in(seeds[2], 2), own, number, SB_DEV, DEVICES, KB, C, 1))(dest_group_keys, dest_group_turns).reshape((SRC_BLOCKS, KB))
    dest_block = with_ends(jax.random.randint(seeds[3], (SRC_BLOCKS, KB), 0, TB_DEV), jax.random.fold_in(seeds[3], 1), 0, TB_DEV - 1).astype(jnp.int32)
    seam_table = draw_seam_table(jax.random.fold_in(seeds[9], 71), 0)
    conv1_weight = noise(seeds[5], (9, HID, FIELDS), (9 * FIELDS) ** -0.5, 0.3125)
    conv1_bias = noise(seeds[6], (HID,), 0.5, 3.0, (), jnp.float32)
    conv2_weight = noise(seeds[7], (9, HID, HID), (9 * HID) ** -0.5, 0.1875)
    conv2_bias = noise(seeds[8], (HID,), 0.5, 3.0, (), jnp.float32)
    return dict(source=source, regrid_weights=regrid_weights, dest_group=dest_group, dest_block=dest_block, seam_table=seam_table, conv1_weight=conv1_weight, conv1_bias=conv1_bias, conv2_weight=conv2_weight, conv2_bias=conv2_bias)


def conv_faces(field_in, weight, bias_row, seam_table):
    channels = field_in.shape[0]
    side_len = field_in.shape[2]
    edge_lines = jnp.stack((field_in[:, :, 0, :], field_in[:, :, -1, :], field_in[:, :, :, 0], field_in[:, :, :, -1]), axis=2).reshape(channels, FACES * 4, side_len)
    line_index = (seam_table[:, :, 0] * 4 + seam_table[:, :, 1]).reshape(-1)
    reverse = (seam_table[:, :, 2] == 1).reshape(-1)[None, :, None]
    seam_lines = edge_lines[:, line_index, :]
    seam_lines = jnp.where(reverse, jnp.flip(seam_lines, axis=2), seam_lines).reshape(channels, FACES, 4, side_len)
    weight_wide = weight.astype(jnp.float32)

    def one_face(face_id):
        face_data = field_in[:, face_id]
        face_lines = seam_lines[:, face_id]
        padded = jnp.pad(face_data, ((0, 0), (1, 1), (1, 1)))
        padded = padded.at[:, 0, 1:-1].set(face_lines[:, 0])
        padded = padded.at[:, -1, 1:-1].set(face_lines[:, 1])
        padded = padded.at[:, 1:-1, 0].set(face_lines[:, 2])
        padded = padded.at[:, 1:-1, -1].set(face_lines[:, 3])
        padded = padded.astype(jnp.float32)
        summed = jnp.zeros((weight.shape[1], side_len, side_len), jnp.float32)
        for row_off in range(3):
            for col_off in range(3):
                window = padded[:, row_off:row_off + side_len, col_off:col_off + side_len]
                summed = summed + jnp.einsum("oi,irc->orc", weight_wide[3 * row_off + col_off], window)
        return jax.nn.gelu(summed + bias_row[:, None, None], approximate=False).astype(jnp.bfloat16)

    out_faces = lax.map(one_face, jnp.arange(FACES, dtype=jnp.int32))
    return jnp.transpose(out_faces, (1, 0, 2, 3))


def reference(source, regrid_weights, dest_group, dest_block, seam_table, conv1_weight, conv1_bias, conv2_weight, conv2_bias):
    devices = N_BAND * N_TILE
    group_blocks = source.reshape(FIELDS, devices, SB_DEV, BLK).transpose(1, 2, 0, 3)
    group_weights = regrid_weights.reshape(devices, SB_DEV, KB, BLK, BLK)

    def one_group(group_pair):
        blocks, weights = group_pair
        return jnp.einsum("sfc,skcd->skfd", blocks.astype(jnp.float32), weights.astype(jnp.float32)).astype(jnp.bfloat16)

    partial_value = lax.map(one_group, (group_blocks, group_weights))
    target = (dest_group * TB_DEV + dest_block).reshape(-1).astype(jnp.int32)
    summed = jax.ops.segment_sum(partial_value.reshape(-1, FIELDS, BLK).astype(jnp.float32), target, num_segments=devices * TB_DEV)
    regridded = summed.reshape(N_BAND, N_TILE, FACES, ROWS_DEV, FIELDS, BLK).transpose(4, 2, 0, 3, 1, 5).reshape(FIELDS, FACES, NSIDE, NSIDE).astype(jnp.bfloat16)
    hidden = conv_faces(regridded, conv1_weight, conv1_bias, seam_table)
    return conv_faces(hidden, conv2_weight, conv2_bias, seam_table)
```

```python
import functools

import jax
import jax.numpy as jnp
import numpy as np
from jax import lax
from jax.experimental import pallas as pl
from jax.experimental.pallas import tpu as pltpu
from jax.sharding import PartitionSpec as P

BF = jnp.bfloat16
F32 = jnp.float32
AXES = ("band", "tile")
VMEM_LIMIT = 56 * 1024 * 1024


def regrid_kernel(pos_ref, src_ref, w_ref, out_ref, *, blocks, top, length):
    step = pl.program_id(0)
    for s in range(blocks):
        lhs = src_ref[:, s * length : (s + 1) * length]
        rhs = jnp.concatenate([w_ref[s, k] for k in range(top)], axis=1)
        val = jnp.dot(lhs, rhs, preferred_element_type=F32).astype(BF)
        for k in range(top):
            where = pos_ref[(step * blocks + s) * top + k]
            out_ref[where] = val[:, k * length : (k + 1) * length]


def regrid(source, weights, position, slots):
    fields = source.shape[0]
    count, top, length = weights.shape[0], weights.shape[1], weights.shape[2]
    blocks = 8
    return pl.pallas_call(
        functools.partial(regrid_kernel, blocks=blocks, top=top, length=length),
        grid_spec=pltpu.PrefetchScalarGridSpec(
            num_scalar_prefetch=1,
            grid=(count // blocks,),
            in_specs=[
                pl.BlockSpec((fields, blocks * length), lambda i, p: (0, i)),
                pl.BlockSpec((blocks, top, length, length), lambda i, p: (i, 0, 0, 0)),
            ],
            out_specs=pl.BlockSpec((slots, fields, length), lambda i, p: (0, 0, 0)),
        ),
        out_shape=jax.ShapeDtypeStruct((slots, fields, length), BF),
        compiler_params=pltpu.CompilerParams(vmem_limit_bytes=VMEM_LIMIT),
        cost_estimate=pl.CostEstimate(
            flops=2 * count * top * length * length * fields, bytes_accessed=17_000_000, transcendentals=0
        ),
    )(position, source, weights)


def place_kernel(slot_ref, in_ref, out_ref, acc_ref, *, chunk):
    step = pl.program_id(0)

    @pl.when(step == 0)
    def _():
        acc_ref[...] = jnp.zeros_like(acc_ref)

    def body(i, carry):
        where = slot_ref[step * chunk + i]
        acc_ref[where] += in_ref[i].astype(F32)
        return carry

    lax.fori_loop(0, chunk, body, 0, unroll=8)

    @pl.when(step == pl.num_programs(0) - 1)
    def _():
        out_ref[...] = acc_ref[: out_ref.shape[0]].astype(BF)


def place(arrived, slots, count):
    items, fields, length = arrived.shape
    chunk = 96
    return pl.pallas_call(
        functools.partial(place_kernel, chunk=chunk),
        grid_spec=pltpu.PrefetchScalarGridSpec(
            num_scalar_prefetch=1,
            grid=(items // chunk,),
            in_specs=[pl.BlockSpec((chunk, fields, length), lambda i, p: (i, 0, 0))],
            out_specs=pl.BlockSpec((count, fields, length), lambda i, p: (0, 0, 0)),
            scratch_shapes=[pltpu.VMEM((count + 1, fields, length), F32)],
        ),
        out_shape=jax.ShapeDtypeStruct((count, fields, length), BF),
        compiler_params=pltpu.CompilerParams(vmem_limit_bytes=VMEM_LIMIT),
    )(slots, arrived)


def gelu(v):
    return 0.5 * v * (1.0 + lax.erf(v * np.float32(1.0 / np.sqrt(2.0))))


def conv_kernel(w_ref, b_ref, x_ref, top_ref, bot_ref, l_ref, r_ref, o_ref, p_ref, s_ref, *, last):
    faces, rows, chans, cols = x_ref.shape
    depth = p_ref.shape[1]
    hid = b_ref.shape[0] // 2
    lane = lax.broadcasted_iota(jnp.int32, (chans, cols), 1)
    spare = depth - 3 * chans
    for f in range(faces):
        left = l_ref[f].astype(F32)
        right = r_ref[f].astype(F32)
        for r in range(rows + 2):
            row = top_ref[f] if r == 0 else bot_ref[f] if r == rows + 1 else x_ref[f, r - 1]
            mid = row.astype(F32)
            lo = jnp.where(lane == 0, left[:, r : r + 1], pltpu.roll(mid, 1, 1))
            hi = jnp.where(lane == cols - 1, right[:, r : r + 1], pltpu.roll(mid, cols - 1, 1))
            parts = [lo, mid, hi]
            if spare:
                parts.append(jnp.zeros((spare, cols), F32))
            p_ref[r, :, f * cols : (f + 1) * cols] = jnp.concatenate(parts, axis=0).astype(BF)
    bias = b_ref[...]
    for rp in range(rows // 2):
        patch = p_ref[2 * rp : 2 * rp + 4].reshape(4 * depth, faces * cols)
        acc = jnp.dot(w_ref[...], patch, preferred_element_type=F32) + bias
        acc = gelu(acc)
        for d in range(2):
            for f in range(faces):
                piece = acc[d * hid : (d + 1) * hid, f * cols : (f + 1) * cols]
                if last:
                    s_ref[f, (2 * rp + d) * hid : (2 * rp + d + 1) * hid, :] = piece
                else:
                    o_ref[f, 2 * rp + d] = piece.astype(BF)
    if last:
        for f in range(faces):
            for o in range(hid):
                o_ref[o, f] = s_ref[f, pl.ds(o, rows, stride=hid), :].astype(BF)


def conv(x, top, bottom, left, right, weight, bias, last):
    face_count, rows, chans, cols = x.shape
    depth = weight.shape[1] // 4
    hid = weight.shape[0] // 2
    faces = 2
    if last:
        out_shape = (hid, face_count, rows, cols)
        out_spec = pl.BlockSpec((hid, faces, rows, cols), lambda i: (0, i, 0, 0))
        scratch = (faces, rows * hid, cols)
    else:
        out_shape = (face_count, rows, hid, cols)
        out_spec = pl.BlockSpec((faces, rows, hid, cols), lambda i: (i, 0, 0, 0))
        scratch = (1, 8, 128)
    return pl.pallas_call(
        functools.partial(conv_kernel, last=last),
        grid=(face_count // faces,),
        in_specs=[
            pl.BlockSpec(weight.shape, lambda i: (0, 0)),
            pl.BlockSpec(bias.shape, lambda i: (0, 0)),
            pl.BlockSpec((faces, rows, chans, cols), lambda i: (i, 0, 0, 0)),
            pl.BlockSpec((faces, chans, cols), lambda i: (i, 0, 0)),
            pl.BlockSpec((faces, chans, cols), lambda i: (i, 0, 0)),
            pl.BlockSpec((faces, chans, rows + 2), lambda i: (i, 0, 0)),
            pl.BlockSpec((faces, chans, rows + 2), lambda i: (i, 0, 0)),
        ],
        out_specs=out_spec,
        out_shape=jax.ShapeDtypeStruct(out_shape, BF),
        scratch_shapes=[pltpu.VMEM((rows + 2, depth, faces * cols), BF), pltpu.VMEM(scratch, F32)],
        compiler_params=pltpu.CompilerParams(vmem_limit_bytes=VMEM_LIMIT),
    )(weight, bias, x, top, bottom, left, right)


def wide_weight(weight, depth):
    taps, hid, chans = weight.shape
    rows = weight.reshape(3, 3, hid, chans).transpose(2, 0, 1, 3).reshape(hid, 3, 3 * chans)
    rows = jnp.pad(rows, ((0, 0), (0, 0), (0, depth - 3 * chans)))
    first = jnp.pad(rows, ((0, 0), (0, 1), (0, 0)))
    second = jnp.pad(rows, ((0, 0), (1, 0), (0, 0)))
    return jnp.stack([first, second]).reshape(2 * hid, 4 * depth)


class Plan:
    def __init__(self, bands, tiles):
        self.bands, self.tiles = bands, tiles
        self.per = bands // tiles
        per, last = self.per, bands - 1
        rounds = per + 1
        count = bands * tiles
        self.pairs = [[] for _ in range(rounds)]
        self.sends_row = np.zeros((rounds, count), np.int32)
        self.unit = np.zeros((rounds, count), np.int32)
        self.row_round = np.full((count, per), rounds, np.int32)
        self.col_round = np.full((count,), rounds, np.int32)

        def join(r, row_dev, col_dev, j):
            if row_dev == col_dev:
                return
            self.pairs[r] += [(row_dev, col_dev), (col_dev, row_dev)]
            self.sends_row[r, row_dev] = 1
            self.unit[r, row_dev] = j
            self.row_round[row_dev, j] = r
            self.col_round[col_dev] = r

        for j in range(per):
            for t in range(tiles):
                join(per if (t, j) == (tiles - 1, 0) else j, t, (per * t + j) * tiles, j)
                join(
                    per if (t, j) == (0, per - 1) else j,
                    last * tiles + t,
                    (per * t + j) * tiles + tiles - 1,
                    j,
                )
        self.self_unit = np.zeros((count,), np.int32)
        self.self_unit[last * tiles + tiles - 1] = per - 1
        for pairs in self.pairs:
            assert len({a for a, _ in pairs}) == len(pairs) == len({b for _, b in pairs})
        self.flip_row = [
            (b * tiles + t, b * tiles + tiles - 1 - t) for b in (0, last) for t in range(tiles)
        ]
        self.flip_col = [(b * tiles + t, (last - b) * tiles + t) for b in range(bands) for t in (0, tiles - 1)]


def seam_tables(seam_table, band, tile):
    line = seam_table[:, :, 1] * seam_table.shape[0] + seam_table[:, :, 0]
    rev = seam_table[:, :, 2] == 1
    row_side = band != 0
    col_side = tile != 0
    row_line = jnp.where(row_side, line[:, 1], line[:, 0])
    row_rev = jnp.where(row_side, rev[:, 1], rev[:, 0])
    col_line = jnp.where(col_side, line[:, 3], line[:, 2])
    col_rev = jnp.where(col_side, rev[:, 3], rev[:, 2])
    lines = jnp.arange(4 * seam_table.shape[0])
    row_hot = (row_line[:, None] == lines[None, :]).astype(BF)
    col_hot = (col_line[:, None] == lines[None, :]).astype(BF)
    return row_hot, row_rev, col_hot, col_rev


def exchange(x, plan, tables):
    faces, rows, chans, cols = x.shape
    bands, tiles, per = plan.bands, plan.tiles, plan.per
    band, tile = lax.axis_index("band"), lax.axis_index("tile")
    me = band * tiles + tile
    row_hot, row_rev, col_hot, col_rev = tables
    first_band, last_band = band == 0, band == bands - 1
    first_tile, last_tile = tile == 0, tile == tiles - 1

    around = [(i, (i + 1) % bands) for i in range(bands)]
    top = lax.ppermute(x[:, rows - 1], "band", around)
    bottom = lax.ppermute(x[:, 0], "band", [(j, i) for i, j in around])
    own_left = jnp.concatenate([top[:, None, :, 0], x[:, :, :, 0], bottom[:, None, :, 0]], axis=1)
    own_right = jnp.concatenate([top[:, None, :, -1], x[:, :, :, -1], bottom[:, None, :, -1]], axis=1)
    across = [(i, (i + 1) % tiles) for i in range(tiles)]
    left = lax.ppermute(own_right, "tile", across)
    right = lax.ppermute(own_left, "tile", [(j, i) for i, j in across])

    col_lines = jnp.where(first_tile, jnp.stack([own_left, left]), jnp.stack([right, own_right]))
    row_a = jnp.where(first_band, x[:, 0], bottom)
    row_b = jnp.where(first_band, top, x[:, rows - 1])
    ends_a = jnp.where(first_band, jnp.stack([left[:, 1], right[:, 1]]), jnp.stack([left[:, rows + 1], right[:, rows + 1]]))
    ends_b = jnp.where(first_band, jnp.stack([left[:, 0], right[:, 0]]), jnp.stack([left[:, rows], right[:, rows]]))
    row_lines = jnp.stack(
        [
            jnp.concatenate([ends[0][:, :, None], line, ends[1][:, :, None]], axis=2)
            for line, ends in ((row_a, ends_a), (row_b, ends_b))
        ]
    )
    row_lines = row_lines.transpose(0, 1, 3, 2)
    units = jnp.stack([row_lines[:, :, rows * j : rows * j + rows + 2] for j in range(per)])

    got = []
    for r, pairs in enumerate(plan.pairs):
        sends_row = jnp.asarray(plan.sends_row[r])[me] == 1
        mine = lax.dynamic_index_in_dim(units, jnp.asarray(plan.unit[r])[me], 0, keepdims=False)
        got.append(lax.ppermute(jnp.where(sends_row, mine, col_lines), AXES, pairs))
    for_col = jnp.stack(got + [lax.dynamic_index_in_dim(units, jnp.asarray(plan.self_unit)[me], 0, keepdims=False)])
    for_row = jnp.stack(got + [col_lines])
    other_rows = lax.dynamic_index_in_dim(for_col, jnp.asarray(plan.col_round)[me], 0, keepdims=False)
    row_round = jnp.asarray(plan.row_round)[me]
    parts = [lax.dynamic_index_in_dim(for_row, row_round[j], 0, keepdims=False) for j in range(per)]
    other_cols = jnp.concatenate(
        [parts[0][:, :, :1]] + [p[:, :, 1 : rows + 1] for p in parts] + [parts[-1][:, :, rows + 1 :]], axis=2
    )

    def select(hot, lines):
        lines = lines.reshape((-1,) + lines.shape[2:])
        return jnp.einsum("fl,lpc->fpc", hot, lines, preferred_element_type=F32).astype(BF)

    def turn(lines):
        n = lines.shape[1]
        back = jnp.asarray(np.eye(n)[::-1].copy(), BF)
        return jnp.einsum("qp,fpc->fqc", back, lines, preferred_element_type=F32).astype(BF)

    sel_row = select(row_hot, jnp.concatenate([row_lines, other_cols]))
    sel_col = select(col_hot, jnp.concatenate([other_rows, col_lines]))
    back_row = turn(lax.ppermute(sel_row, AXES, plan.flip_row))
    back_col = turn(lax.ppermute(sel_col, AXES, plan.flip_col))
    seam_row = jnp.where(row_rev[:, None, None], back_row, sel_row)
    seam_col = jnp.where(col_rev[:, None, None], back_col, sel_col)

    place = jnp.arange(rows + 2)
    corner = (first_band & (place == 0)) | (last_band & (place == rows + 1))
    seam_col = jnp.where(corner[None, :, None], jnp.zeros_like(seam_col), seam_col)
    left = jnp.where(first_tile, seam_col, left)
    right = jnp.where(last_tile, seam_col, right)

    def ends(col, side, on_seam, at_end):
        end = seam_row[:, 0 if side == 0 else cols + 1]
        end = jnp.where(at_end, jnp.zeros_like(end), end)
        low = jnp.where(first_band, end, col[:, 0])
        high = jnp.where(last_band, end, col[:, rows + 1])
        return jnp.concatenate([low[:, None], col[:, 1 : rows + 1], high[:, None]], axis=1)

    left = ends(left, 0, None, first_tile)
    right = ends(right, 1, None, last_tile)
    seam_mid = seam_row[:, 1 : cols + 1].transpose(0, 2, 1)
    top = jnp.where(first_band, seam_mid, top)
    bottom = jnp.where(last_band, seam_mid, bottom)
    return top, bottom, left.transpose(0, 2, 1), right.transpose(0, 2, 1)


def local(
    source,
    regrid_weights,
    dest_group,
    dest_block,
    seam_table,
    conv1_weight,
    conv1_bias,
    conv2_weight,
    conv2_bias,
):
    bands, tiles = lax.axis_size("band"), lax.axis_size("tile")
    devices = bands * tiles
    src_count, top_count, block_len = regrid_weights.shape[:3]
    capacity = 3 * src_count * top_count // devices
    rows = block_len * tiles // bands
    faces = seam_table.shape[0]
    slots_dev = faces * rows
    fields = source.shape[0]
    hid = conv1_weight.shape[1]
    items = src_count * top_count
    total = devices * capacity

    target = dest_group.reshape(items)
    order = jnp.arange(items)
    same = (target[:, None] == target[None, :]) & (order[None, :] < order[:, None])
    position = target * capacity + jnp.sum(same.astype(jnp.int32), axis=1)
    hit = position[:, None] == jnp.arange(total)[None, :]
    out_slots = slots_dev + jnp.sum(
        jnp.where(hit, (dest_block.reshape(items) - slots_dev)[:, None], 0), axis=0
    )
    slots = lax.all_to_all(out_slots.reshape(devices, capacity), AXES, split_axis=0, concat_axis=0, tiled=True)
    outgoing = regrid(source, regrid_weights, position, total)
    arrived = lax.all_to_all(
        outgoing.reshape(devices, capacity, fields, block_len), AXES, split_axis=0, concat_axis=0, tiled=True
    )
    regridded = place(arrived.reshape(total, fields, block_len), slots.reshape(total), slots_dev)
    regridded = regridded.reshape(faces, rows, fields, block_len)

    plan = Plan(bands, tiles)
    tables = seam_tables(seam_table, lax.axis_index("band"), lax.axis_index("tile"))
    depth1 = -(-3 * fields // 128) * 128
    weight1 = wide_weight(conv1_weight, depth1)
    weight2 = wide_weight(conv2_weight, 3 * hid)
    bias1 = jnp.concatenate([conv1_bias, conv1_bias])[:, None]
    bias2 = jnp.concatenate([conv2_bias, conv2_bias])[:, None]
    hidden = conv(regridded, *exchange(regridded, plan, tables), weight1, bias1, False)
    return conv(hidden, *exchange(hidden, plan, tables), weight2, bias2, True)


def solution(mesh):
    return jax.shard_map(
        local,
        mesh=mesh,
        in_specs=(
            P(None, AXES),
            P(AXES, None, None, None),
            P(AXES, None),
            P(AXES, None),
            P(),
            P(),
            P(),
            P(),
            P(),
        ),
        out_specs=P(None, None, "band", "tile"),
        check_vma=False,
    )
```

```python
import functools

import jax
import jax.numpy as jnp
import numpy as np
from jax import lax
from jax.experimental import pallas as pl
from jax.experimental.pallas import tpu as pltpu
from jax.sharding import PartitionSpec as P

BF = jnp.bfloat16
F32 = jnp.float32
AXES = ("band", "tile")
VMEM_LIMIT = 56 * 1024 * 1024


def regrid_kernel(pos_ref, src_ref, w_ref, out_ref, *, blocks, top, length):
    step = pl.program_id(0)
    for s in range(blocks):
        lhs = src_ref[:, s * length : (s + 1) * length]
        rhs = jnp.concatenate([w_ref[s, k] for k in range(top)], axis=1)
        val = jnp.dot(lhs, rhs, preferred_element_type=F32).astype(BF)
        for k in range(top):
            where = pos_ref[(step * blocks + s) * top + k]
            out_ref[where] = val[:, k * length : (k + 1) * length]


def regrid(source, weights, position, slots):
    fields = source.shape[0]
    count, top, length = weights.shape[0], weights.shape[1], weights.shape[2]
    blocks = 8
    return pl.pallas_call(
        functools.partial(regrid_kernel, blocks=blocks, top=top, length=length),
        grid_spec=pltpu.PrefetchScalarGridSpec(
            num_scalar_prefetch=1,
            grid=(count // blocks,),
            in_specs=[
                pl.BlockSpec((fields, blocks * length), lambda i, p: (0, i)),
                pl.BlockSpec((blocks, top, length, length), lambda i, p: (i, 0, 0, 0)),
            ],
            out_specs=pl.BlockSpec((slots, fields, length), lambda i, p: (0, 0, 0)),
        ),
        out_shape=jax.ShapeDtypeStruct((slots, fields, length), BF),
        compiler_params=pltpu.CompilerParams(vmem_limit_bytes=VMEM_LIMIT),
        cost_estimate=pl.CostEstimate(
            flops=2 * count * top * length * length * fields, bytes_accessed=17_000_000, transcendentals=0
        ),
    )(position, source, weights)


def edge_columns(piece, lane, at, low, high):
    cols = piece.shape[1]
    here = lane == at
    low = jnp.where(here, pltpu.roll(piece, at, 1) if at else piece, low)
    high = jnp.where(here, pltpu.roll(piece, (at + 1) % cols, 1), high)
    return low, high


def place_kernel(slot_ref, in_ref, out_ref, low_ref, high_ref, acc_ref, *, chunk):
    step = pl.program_id(0)

    @pl.when(step == 0)
    def _():
        acc_ref[...] = jnp.zeros_like(acc_ref)

    def body(i, carry):
        where = slot_ref[step * chunk + i]
        acc_ref[where] += in_ref[i].astype(F32)
        return carry

    lax.fori_loop(0, chunk, body, 0, unroll=8)

    @pl.when(step == pl.num_programs(0) - 1)
    def _():
        count, chans, cols = out_ref.shape
        lane = lax.broadcasted_iota(jnp.int32, (chans, cols), 1)
        for half in range(2):
            low = high = jnp.zeros((chans, cols), F32)
            for at in range(min(cols, count - half * cols)):
                piece = acc_ref[half * cols + at]
                out_ref[half * cols + at] = piece.astype(BF)
                low, high = edge_columns(piece, lane, at, low, high)
            low_ref[:, half * cols : (half + 1) * cols] = low.astype(BF)
            high_ref[:, half * cols : (half + 1) * cols] = high.astype(BF)


def place(arrived, slots, count):
    items, fields, length = arrived.shape
    chunk = 96
    return pl.pallas_call(
        functools.partial(place_kernel, chunk=chunk),
        grid_spec=pltpu.PrefetchScalarGridSpec(
            num_scalar_prefetch=1,
            grid=(items // chunk,),
            in_specs=[pl.BlockSpec((chunk, fields, length), lambda i, p: (i, 0, 0))],
            out_specs=[
                pl.BlockSpec((count, fields, length), lambda i, p: (0, 0, 0)),
                pl.BlockSpec((fields, 2 * length), lambda i, p: (0, 0)),
                pl.BlockSpec((fields, 2 * length), lambda i, p: (0, 0)),
            ],
            scratch_shapes=[pltpu.VMEM((count + 1, fields, length), F32)],
        ),
        out_shape=[
            jax.ShapeDtypeStruct((count, fields, length), BF),
            jax.ShapeDtypeStruct((fields, 2 * length), BF),
            jax.ShapeDtypeStruct((fields, 2 * length), BF),
        ],
        compiler_params=pltpu.CompilerParams(vmem_limit_bytes=VMEM_LIMIT),
    )(slots, arrived)


def gelu(v):
    return 0.5 * v * (1.0 + lax.erf(v * np.float32(1.0 / np.sqrt(2.0))))


def conv_kernel(w_ref, b_ref, x_ref, top_ref, bot_ref, l_ref, r_ref, *refs, last):
    if last:
        o_ref, p_ref, s_ref = refs
    else:
        o_ref, low_ref, high_ref, p_ref = refs
    faces, rows, chans, cols = x_ref.shape
    depth = p_ref.shape[1]
    hid = b_ref.shape[0] // 2
    step = pl.program_id(0)
    lane = lax.broadcasted_iota(jnp.int32, (chans, cols), 1)
    spare = depth - 3 * chans
    span = rows + 2
    group = pl.ds(pl.multiple_of((step // 3) * cols, cols), cols)
    back = lax.rem(cols - lax.rem(step, 3) * (faces * span), cols)
    left = pltpu.roll(l_ref[:, group].astype(F32), back, 1)
    right = pltpu.roll(r_ref[:, group].astype(F32), back, 1)
    for f in range(faces):
        for r in range(span):
            row = top_ref[f] if r == 0 else bot_ref[f] if r == rows + 1 else x_ref[f, r - 1]
            mid = row.astype(F32)
            at = f * span + r
            lo = jnp.where(lane == 0, left[:, at : at + 1], pltpu.roll(mid, 1, 1))
            hi = jnp.where(lane == cols - 1, right[:, at : at + 1], pltpu.roll(mid, cols - 1, 1))
            parts = [lo, mid, hi]
            if spare:
                parts.append(jnp.zeros((spare, cols), F32))
            p_ref[r, :, f * cols : (f + 1) * cols] = jnp.concatenate(parts, axis=0).astype(BF)
    bias = b_ref[...]
    out_lane = lax.broadcasted_iota(jnp.int32, (hid, cols), 1)
    low = high = jnp.zeros((hid, cols), F32)
    for rp in range(rows // 2):
        patch = p_ref[2 * rp : 2 * rp + 4].reshape(4 * depth, faces * cols)
        acc = jnp.dot(w_ref[...], patch, preferred_element_type=F32) + bias
        acc = gelu(acc)
        for d in range(2):
            for f in range(faces):
                piece = acc[d * hid : (d + 1) * hid, f * cols : (f + 1) * cols]
                if last:
                    s_ref[f, (2 * rp + d) * hid : (2 * rp + d + 1) * hid, :] = piece
                else:
                    o_ref[f, 2 * rp + d] = piece.astype(BF)
                    low, high = edge_columns(piece, out_lane, f * rows + 2 * rp + d, low, high)
    if last:
        for f in range(faces):
            for o in range(hid):
                o_ref[o, f] = s_ref[f, pl.ds(o, rows, stride=hid), :].astype(BF)
    else:
        per = cols // (faces * rows)
        ahead = lax.rem(step, per) * (faces * rows)
        half = pl.ds(pl.multiple_of((step // per) * cols, cols), cols)
        fresh = lax.rem(step, per) == 0
        for ref, value in ((low_ref, low), (high_ref, high)):
            value = pltpu.roll(value, ahead, 1).astype(BF)

            @pl.when(fresh)
            def _(ref=ref, value=value):
                ref[:, half] = value

            @pl.when(jnp.logical_not(fresh))
            def _(ref=ref, value=value):
                ref[:, half] += value


def conv(x, top, bottom, left, right, weight, bias, last):
    face_count, rows, chans, cols = x.shape
    depth = weight.shape[1] // 4
    hid = weight.shape[0] // 2
    faces = 2
    scratch = [pltpu.VMEM((rows + 2, depth, faces * cols), BF)]
    if last:
        out_shape = jax.ShapeDtypeStruct((hid, face_count, rows, cols), BF)
        out_spec = pl.BlockSpec((hid, faces, rows, cols), lambda i: (0, i, 0, 0))
        scratch.append(pltpu.VMEM((faces, rows * hid, cols), F32))
    else:
        out_shape = [jax.ShapeDtypeStruct((face_count, rows, hid, cols), BF)]
        out_shape += [jax.ShapeDtypeStruct((hid, 2 * cols), BF)] * 2
        out_spec = [pl.BlockSpec((faces, rows, hid, cols), lambda i: (i, 0, 0, 0))]
        out_spec += [pl.BlockSpec((hid, 2 * cols), lambda i: (0, 0))] * 2
    return pl.pallas_call(
        functools.partial(conv_kernel, last=last),
        grid=(face_count // faces,),
        in_specs=[
            pl.BlockSpec(weight.shape, lambda i: (0, 0)),
            pl.BlockSpec(bias.shape, lambda i: (0, 0)),
            pl.BlockSpec((faces, rows, chans, cols), lambda i: (i, 0, 0, 0)),
            pl.BlockSpec((faces, chans, cols), lambda i: (i, 0, 0)),
            pl.BlockSpec((faces, chans, cols), lambda i: (i, 0, 0)),
            pl.BlockSpec(left.shape, lambda i: (0, 0)),
            pl.BlockSpec(right.shape, lambda i: (0, 0)),
        ],
        out_specs=out_spec,
        out_shape=out_shape,
        scratch_shapes=scratch,
        compiler_params=pltpu.CompilerParams(vmem_limit_bytes=VMEM_LIMIT),
    )(weight, bias, x, top, bottom, left, right)


def wide_weight(weight, depth):
    taps, hid, chans = weight.shape
    rows = weight.reshape(3, 3, hid, chans).transpose(2, 0, 1, 3).reshape(hid, 3, 3 * chans)
    rows = jnp.pad(rows, ((0, 0), (0, 0), (0, depth - 3 * chans)))
    first = jnp.pad(rows, ((0, 0), (0, 1), (0, 0)))
    second = jnp.pad(rows, ((0, 0), (1, 0), (0, 0)))
    return jnp.stack([first, second]).reshape(2 * hid, 4 * depth)


class Plan:
    def __init__(self, bands, tiles):
        self.bands, self.tiles = bands, tiles
        self.per = bands // tiles
        per, last = self.per, bands - 1
        rounds = per + 1
        count = bands * tiles
        self.pairs = [[] for _ in range(rounds)]
        self.sends_row = np.zeros((rounds, count), np.int32)
        self.unit = np.zeros((rounds, count), np.int32)
        self.row_round = np.full((count, per), rounds, np.int32)
        self.col_round = np.full((count,), rounds, np.int32)

        def join(r, row_dev, col_dev, j):
            if row_dev == col_dev:
                self.sends_row[r, row_dev] = 1
                return
            self.pairs[r] += [(row_dev, col_dev), (col_dev, row_dev)]
            self.sends_row[r, row_dev] = 1
            self.unit[r, row_dev] = j
            self.row_round[row_dev, j] = r
            self.col_round[col_dev] = r

        for j in range(per):
            for t in range(tiles):
                join(per if (t, j) == (tiles - 1, 0) else j, t, (per * t + j) * tiles, j)
                join(
                    per if (t, j) == (0, per - 1) else j,
                    last * tiles + t,
                    (per * t + j) * tiles + tiles - 1,
                    j,
                )
        for pairs in self.pairs:
            assert len({a for a, _ in pairs}) == len(pairs) == len({b for _, b in pairs})
        self.flip_row = [
            (b * tiles + t, b * tiles + tiles - 1 - t) for b in (0, last) for t in range(tiles)
        ]
        self.flip_col = [(b * tiles + t, (last - b) * tiles + t) for b in range(bands) for t in (0, tiles - 1)]


def lane18(f, p, span, width):
    return (f // 6) * width + (f % 6) * span + p


def fixed_maps(faces, rows, cols):
    span = rows + 2
    own = np.zeros((3 * cols, 2 * cols), np.float32)
    wrap = np.zeros((4 * cols, 2 * cols), np.float32)
    widen = np.zeros((2 * cols, 2 * cols), np.float32)
    ends = np.zeros((2, 2 * cols, 2 * cols), np.float32)
    corner = np.zeros((2, 4 * cols, cols), np.float32)
    unit_ends = np.zeros((2, 2 * cols, 4 * cols), np.float32)
    for f in range(faces):
        for r in range(rows):
            to = lane18(f, r + 1, span, cols)
            own[f * rows + r, to] = wrap[f * rows + r, to] = widen[f * rows + r, to] = 1
        for which, p in ((0, 0), (1, span - 1)):
            to = lane18(f, p, span, cols)
            own[2 * cols + 16 * which + f, to] = 1
            wrap[(2 + which) * cols + 2 * f, to] = 1
            for side in range(2):
                ends[side, which * cols + 2 * f + side, to] = 1
        for which, r in ((0, 0), (1, rows - 1)):
            for side in range(2):
                corner[which, side * 2 * cols + f * rows + r, 2 * f + side] = 1
        for which, p in ((0, 0), (1, span - 1)):
            for pair in range(2):
                to = pair * 2 * cols + lane18(f, p, span, cols)
                unit_ends[which, pair * cols + 2 * f + which, to] = 1
    back = np.eye(cols)[::-1].copy()
    return [jnp.asarray(m, BF) for m in (own, wrap, widen, ends, corner, unit_ends, back)]


def seam_tables(seam_table, plan, rows, cols):
    band, tile = lax.axis_index("band"), lax.axis_index("tile")
    me = band * plan.tiles + tile
    faces = seam_table.shape[0]
    span = rows + 2
    per, rounds = plan.per, plan.per + 1
    last_band, last_tile = plan.bands - 1, plan.tiles - 1
    static = np.concatenate(
        [
            plan.col_round[:, None],
            np.where(plan.row_round[:, :1] == 0, 0, np.where(plan.row_round[:, :1] == per, 1, 2)),
            np.where(plan.row_round[:, -1:] == per - 1, 0, np.where(plan.row_round[:, -1:] == per, 1, 2)),
            plan.sends_row.T + plan.sends_row.T * (plan.unit.T > 0) * (np.arange(rounds) == per),
        ],
        axis=1,
    ).astype(np.int32)
    static = lax.dynamic_slice_in_dim(jnp.asarray(static), me, 1, 0)[0]
    row = jnp.where(band == 0, seam_table[:, 0], seam_table[:, 1])
    col = jnp.where(tile == 0, seam_table[:, 2], seam_table[:, 3])
    scalars = jnp.concatenate(
        [jnp.stack([band, tile]).astype(jnp.int32), static, row[:, 1], row[:, 0], row[:, 2], jnp.zeros((4,), jnp.int32)]
    )
    lanes = np.full((2, 2 * cols), -1, np.int32)
    for f in range(faces):
        for p in range(span):
            lanes[:, lane18(f, p, span, cols)] = f, p
    face, place = lanes
    line_in = np.concatenate([np.where(face >= 0, face + faces * side, -1) for side in range(4)])
    place_in = np.tile(place, 4)
    col_line = col[:, 1] * faces + col[:, 0]
    hot = jnp.asarray(face[:, None] == np.arange(faces)[None, :])
    want = jnp.sum(jnp.where(hot, col_line[None, :], 0), axis=1)
    turned = jnp.sum(jnp.where(hot, col[:, 2][None, :], 0), axis=1)
    pick = (jnp.asarray(line_in)[:, None] == want[None, :]) & jnp.asarray(
        (place_in[:, None] == place[None, :]) & (face >= 0)[None, :]
    )
    corner = ((band == 0) & jnp.asarray(place == 0)) | ((band == last_band) & jnp.asarray(place == span - 1))
    same_face = (face[:, None] == face[None, :]) & (face >= 0)[None, :]
    keep = jnp.asarray(same_face & (place[:, None] == place[None, :])) & (turned == 0)[None, :]
    flip = jnp.asarray(same_face & (place[:, None] == span - 1 - place[None, :])) & (turned == 1)[None, :]
    join = jnp.concatenate([keep, flip]) & jnp.logical_not(corner)[None, :]
    at = np.arange(cols)
    end_face, end_side = np.where(at < 2 * faces, at // 2, -1), at % 2
    end_turned = jnp.sum(jnp.where(jnp.asarray(end_face[:, None] == np.arange(faces)[None, :]), row[:, 2][None, :], 0), axis=1)
    outer = ((tile == 0) & jnp.asarray(end_side == 0)) | ((tile == last_tile) & jnp.asarray(end_side == 1))
    same_end = (end_face[:, None] == end_face[None, :]) & (end_face >= 0)[None, :]
    keep_end = jnp.asarray(same_end & (end_side[:, None] == end_side[None, :])) & (end_turned == 0)[None, :]
    flip_end = jnp.asarray(same_end & (end_side[:, None] != end_side[None, :])) & (end_turned == 1)[None, :]
    join_end = jnp.concatenate([keep_end, flip_end]) & jnp.logical_not(outer)[None, :]
    return scalars, pick.astype(BF), join.astype(BF), join_end.astype(BF), fixed_maps(faces, rows, cols)


BAND, TILE, COL_ROUND, FIRST_FROM, LAST_FROM, SENDS = 0, 1, 2, 3, 4, 5


def whole(kernel, out_shape, scratch, scalars, *args):
    return pl.pallas_call(
        kernel,
        in_specs=[pl.BlockSpec(memory_space=pltpu.SMEM)] + [pl.BlockSpec(memory_space=pltpu.VMEM)] * len(args),
        out_specs=[pl.BlockSpec(memory_space=pltpu.VMEM)] * len(out_shape),
        out_shape=[jax.ShapeDtypeStruct(s, BF) for s in out_shape],
        scratch_shapes=scratch,
        compiler_params=pltpu.CompilerParams(vmem_limit_bytes=VMEM_LIMIT),
    )(scalars, *args)


def pick2(cond, a, b):
    return lax.select_n(cond, b, a)


def side_by_side(*parts):
    return jnp.concatenate(parts, axis=1)


def move(x, matrix):
    return jnp.dot(x, matrix, preferred_element_type=F32)


def rows_kernel(first_ref, last_ref, left_ref, right_ref, corner_ref, up_ref, down_ref):
    faces = first_ref.shape[0]
    both = side_by_side(left_ref[...], right_ref[...])
    for which, (src, out) in enumerate(((first_ref, up_ref), (last_ref, down_ref))):
        for f in range(faces):
            out[f] = src[f, 0]
        out[faces] = move(both, corner_ref[which]).astype(BF)


def rows_call(x, left, right, corner):
    faces, rows, chans, cols = x.shape
    full = lambda a: pl.BlockSpec(a.shape, lambda i: (0,) * a.ndim)
    out = jax.ShapeDtypeStruct((faces + 1, chans, cols), BF)
    return pl.pallas_call(
        rows_kernel,
        grid=(1,),
        in_specs=[
            pl.BlockSpec((faces, 1, chans, cols), lambda i: (0, 0, 0, 0)),
            pl.BlockSpec((faces, 1, chans, cols), lambda i: (0, rows - 1, 0, 0)),
            full(left),
            full(right),
            full(corner),
        ],
        out_specs=[pl.BlockSpec(out.shape, lambda i: (0, 0, 0))] * 2,
        out_shape=[out] * 2,
        compiler_params=pltpu.CompilerParams(vmem_limit_bytes=VMEM_LIMIT),
    )(x, x, left, right, corner)


def lines_kernel(s_ref, up_ref, down_ref, top_ref, bot_ref, low_ref, high_ref, left_ref, right_ref, own_ref, wrap_ref, ue_ref, *outs, bands, rows):
    messages, cl_ref = outs[:-1], outs[-1]
    per = len(messages) - 1
    faces, (chans, cols) = up_ref.shape[0] - 1, up_ref.shape[1:]
    span = rows + 2
    first_band, first_tile = s_ref[BAND] == 0, s_ref[TILE] == 0
    lane = lax.broadcasted_iota(jnp.int32, (chans, cols), 1)
    top_edge = jnp.zeros((chans, cols), F32)
    for which, ref in enumerate((top_ref, bot_ref)):
        for f in range(faces):
            at = 16 * which + f
            row = ref[f].astype(F32)
            value = pltpu.roll(row, pick2(first_tile, jnp.int32(at), jnp.int32(at + 1)), 1)
            top_edge = jnp.where(lane == at, value, top_edge)
    mine = pick2(first_tile, low_ref[...], high_ref[...])
    theirs = pick2(first_tile, left_ref[...], right_ref[...])
    turn = pick2(first_tile, jnp.int32(0), jnp.int32(cols - 1))
    tc = pltpu.roll(top_ref[faces].astype(F32), turn, 1).astype(BF)
    bc = pltpu.roll(bot_ref[faces].astype(F32), turn, 1).astype(BF)
    own = move(side_by_side(mine, top_edge.astype(BF)), own_ref[...]).astype(BF)
    wrap = move(side_by_side(theirs, tc, bc), wrap_ref[...]).astype(BF)
    cl_ref[...] = side_by_side(pick2(first_tile, own, wrap), pick2(first_tile, wrap, own))
    on_row = jnp.logical_or(first_band, s_ref[BAND] == bands - 1)
    for m in range(per + 1):

        @pl.when(s_ref[SENDS + m] == 0)
        def _(m=m):
            messages[m][...] = cl_ref[...]

    @pl.when(on_row)
    def _():
        ends = side_by_side(pick2(first_band, up_ref[faces], bot_ref[faces]), pick2(first_band, top_ref[faces], down_ref[faces]))
        for g in range(4):
            pieces = [jnp.zeros((chans, cols), F32) for _ in range(per)]
            for i in range(6):
                pair, f = divmod(6 * g + i, faces)
                line = pick2(first_band, up_ref[f], bot_ref[f]) if pair == 0 else pick2(first_band, top_ref[f], down_ref[f])
                line = line.astype(F32)
                for j in range(per):
                    low = i * span + (1 if j == 0 else 0)
                    high = i * span + span - (1 if j == per - 1 else 0)
                    value = pltpu.roll(line, (i * span + 1 - rows * j) % cols, 1)
                    pieces[j] = jnp.where((lane >= low) & (lane < high), value, pieces[j])
            where = slice(g * cols, (g + 1) * cols)
            for j in (0, per - 1):
                pieces[j] = pieces[j] + move(ends, ue_ref[0 if j == 0 else 1, :, where])
            for j in range(per):

                @pl.when(s_ref[SENDS + j] == 1)
                def _(j=j, piece=pieces[j]):
                    messages[j][:, where] = piece.astype(BF)

            @pl.when(s_ref[SENDS + per] == 1)
            def _(piece=pieces[0]):
                messages[per][:, where] = piece.astype(BF)

            @pl.when(s_ref[SENDS + per] == 2)
            def _(piece=pieces[per - 1]):
                messages[per][:, where] = piece.astype(BF)


def seams_kernel(s_ref, *refs, rounds, rows, bands):
    got, refs = refs[:rounds], refs[rounds:]
    first_msg, last_msg, cl_ref, up_ref, down_ref, top_ref, bot_ref, pick_ref, srow_ref, scol_ref = refs[:10]
    rows_ref, unit0_ref, unit7_ref, other_ref, corner_ref = refs[10:]
    faces, (chans, cols) = up_ref.shape[0] - 1, up_ref.shape[1:]
    per = rounds - 1
    span = rows + 2
    first_band = s_ref[BAND] == 0
    lane = lax.broadcasted_iota(jnp.int32, (chans, cols), 1)
    for r in range(rounds):

        @pl.when(s_ref[COL_ROUND] == r)
        def _(r=r):
            other_ref[...] = got[r][...]

    @pl.when((s_ref[COL_ROUND] == rounds) & first_band)
    def _():
        other_ref[...] = first_msg[...]

    @pl.when((s_ref[COL_ROUND] == rounds) & jnp.logical_not(first_band))
    def _():
        other_ref[...] = last_msg[...]

    scol_ref[...] = move(side_by_side(other_ref[...], cl_ref[...]), pick_ref[...]).astype(BF)

    on_row = jnp.logical_or(first_band, s_ref[BAND] == bands - 1)
    table = SENDS + rounds

    @pl.when(on_row)
    def _():
        for code, to, normal in ((FIRST_FROM, unit0_ref, got[0]), (LAST_FROM, unit7_ref, got[per - 1])):
            for value, src in enumerate((normal, got[per], cl_ref)):

                @pl.when(s_ref[code] == value)
                def _(to=to, src=src):
                    to[...] = src[...]

        for f in range(faces + 1):
            rows_ref[f] = pick2(first_band, up_ref[f], bot_ref[f])
            rows_ref[faces + 1 + f] = pick2(first_band, top_ref[f], down_ref[f])
        units = [unit0_ref, *got[1 : per - 1], unit7_ref]
        corner_ref[...] = jnp.zeros_like(corner_ref)
        for f in range(faces):
            side, face = s_ref[table + f], s_ref[table + faces + f]

            @pl.when(side < 2)
            def _(f=f, side=side, face=face):
                srow_ref[f] = rows_ref[side * (faces + 1) + face]
                ends = rows_ref[side * (faces + 1) + faces].astype(F32)
                ends = pltpu.roll(ends, lax.rem(2 * f + 2 * cols - 2 * face, cols), 1)
                corner_ref[...] = jnp.where((lane == 2 * f) | (lane == 2 * f + 1), ends, corner_ref[...])

            @pl.when(side >= 2)
            def _(f=f, side=side, face=face):
                group = pl.ds(pl.multiple_of(((side - 2) * 2 + face // 6) * cols, cols), cols)
                q = lax.rem(face, 6) * span
                line = jnp.zeros((chans, cols), F32)
                ends = corner_ref[...]
                for j in range(per):
                    value = units[j][:, group].astype(F32)
                    line = jnp.where(lane // rows == j, pltpu.roll(value, lax.rem(rows * j + 2 * cols - 1 - q, cols), 1), line)
                    if j == 0:
                        ends = jnp.where(lane == 2 * f, pltpu.roll(value, lax.rem(2 * f + 2 * cols - q, cols), 1), ends)
                    if j == per - 1:
                        shift = lax.rem(2 * f + 1 + 2 * cols - q - (span - 1), cols)
                        ends = jnp.where(lane == 2 * f + 1, pltpu.roll(value, shift, 1), ends)
                srow_ref[f] = line.astype(BF)
                corner_ref[...] = ends

        srow_ref[faces] = corner_ref[...].astype(BF)

    @pl.when(jnp.logical_not(on_row))
    def _():
        srow_ref[...] = jnp.zeros_like(srow_ref)


def halo_kernel(s_ref, srow_ref, rrow_ref, scol_ref, rcol_ref, top_ref, bot_ref, left_ref, right_ref, join_ref, joinend_ref, back_ref, widen_ref, ends_ref, t_out, b_out, l_out, r_out, *, bands, tiles, rounds):
    faces, (chans, cols) = top_ref.shape[0] - 1, top_ref.shape[1:]
    first_band, last_band = s_ref[BAND] == 0, s_ref[BAND] == bands - 1
    first_tile, last_tile = s_ref[TILE] == 0, s_ref[TILE] == tiles - 1
    table = SENDS + rounds + 2 * faces
    for cond, out, ref in ((first_band, t_out, top_ref), (last_band, b_out, bot_ref)):

        @pl.when(cond)
        def _(out=out):
            for f in range(faces):
                turned = move(rrow_ref[f], back_ref[...]).astype(BF)
                out[f] = pick2(s_ref[table + f] == 1, turned, srow_ref[f])

        @pl.when(jnp.logical_not(cond))
        def _(out=out, ref=ref):
            for f in range(faces):
                out[f] = ref[f]

    ends = move(side_by_side(srow_ref[faces], rrow_ref[faces]), joinend_ref[...]).astype(BF)
    top_end = pick2(first_band, ends, top_ref[faces])
    bot_end = pick2(last_band, ends, bot_ref[faces])
    none = jnp.zeros_like(top_end)
    seam = move(side_by_side(scol_ref[...], rcol_ref[...]), join_ref[...])
    for side, (at_edge, src, out) in enumerate(((first_tile, left_ref, l_out), (last_tile, right_ref, r_out))):
        use_top = jnp.logical_or(first_band, jnp.logical_not(at_edge))
        use_bot = jnp.logical_or(last_band, jnp.logical_not(at_edge))
        both = side_by_side(pick2(use_top, top_end, none), pick2(use_bot, bot_end, none))
        base = pick2(at_edge, seam, move(src[...], widen_ref[...]))
        out[...] = (base + move(both, ends_ref[side])).astype(BF)


def exchange(x, low, high, plan, tables):
    scalars, pick, join, join_end, (own, wrap, widen, ends, corner, unit_ends, back) = tables
    faces, rows, chans, cols = x.shape
    bands, tiles = plan.bands, plan.tiles
    rounds = len(plan.pairs)
    across = [(i, (i + 1) % tiles) for i in range(tiles)]
    left = lax.ppermute(high, "tile", across)
    right = lax.ppermute(low, "tile", [(j, i) for i, j in across])
    up, down = rows_call(x, left, right, corner)
    around = [(i, (i + 1) % bands) for i in range(bands)]
    top = lax.ppermute(down, "band", around)
    bottom = lax.ppermute(up, "band", [(j, i) for i, j in around])
    outs = whole(
        functools.partial(lines_kernel, bands=bands, rows=rows),
        [(chans, 4 * cols)] * (rounds + 1),
        [],
        scalars, up, down, top, bottom, low, high, left, right, own, wrap, unit_ends,
    )
    messages, col_lines = outs[:-1], outs[-1]
    got = [lax.ppermute(m, AXES, pairs) for m, pairs in zip(messages, plan.pairs)]
    line = (faces + 1, chans, cols)
    srow, scol = whole(
        functools.partial(seams_kernel, rounds=rounds, rows=rows, bands=bands),
        [line, (chans, 2 * cols)],
        [
            pltpu.VMEM((2 * (faces + 1), chans, cols), BF),
            pltpu.VMEM((chans, 4 * cols), BF),
            pltpu.VMEM((chans, 4 * cols), BF),
            pltpu.VMEM((chans, 4 * cols), BF),
            pltpu.VMEM((chans, cols), F32),
        ],
        scalars, *got, messages[0], messages[plan.per - 1], col_lines, up, down, top, bottom, pick,
    )
    rrow = lax.ppermute(srow, AXES, plan.flip_row)
    rcol = lax.ppermute(scol, AXES, plan.flip_col)
    rim = (faces, chans, cols)
    return whole(
        functools.partial(halo_kernel, bands=bands, tiles=tiles, rounds=rounds),
        [rim, rim, (chans, 2 * cols), (chans, 2 * cols)],
        [],
        scalars, srow, rrow, scol, rcol, top, bottom, left, right, join, join_end, back, widen, ends,
    )


def local(
    source,
    regrid_weights,
    dest_group,
    dest_block,
    seam_table,
    conv1_weight,
    conv1_bias,
    conv2_weight,
    conv2_bias,
):
    bands, tiles = lax.axis_size("band"), lax.axis_size("tile")
    devices = bands * tiles
    src_count, top_count, block_len = regrid_weights.shape[:3]
    capacity = 3 * src_count * top_count // devices
    rows = block_len * tiles // bands
    faces = seam_table.shape[0]
    slots_dev = faces * rows
    fields = source.shape[0]
    hid = conv1_weight.shape[1]
    items = src_count * top_count
    total = devices * capacity

    target = dest_group.reshape(items)
    order = jnp.arange(items)
    same = (target[:, None] == target[None, :]) & (order[None, :] < order[:, None])
    position = target * capacity + jnp.sum(same.astype(jnp.int32), axis=1)
    hit = position[:, None] == jnp.arange(total)[None, :]
    out_slots = slots_dev + jnp.sum(
        jnp.where(hit, (dest_block.reshape(items) - slots_dev)[:, None], 0), axis=0
    )
    slots = lax.all_to_all(out_slots.reshape(devices, capacity), AXES, split_axis=0, concat_axis=0, tiled=True)
    outgoing = regrid(source, regrid_weights, position, total)
    arrived = lax.all_to_all(
        outgoing.reshape(devices, capacity, fields, block_len), AXES, split_axis=0, concat_axis=0, tiled=True
    )
    regridded, low, high = place(arrived.reshape(total, fields, block_len), slots.reshape(total), slots_dev)
    regridded = regridded.reshape(faces, rows, fields, block_len)

    plan = Plan(bands, tiles)
    tables = seam_tables(seam_table, plan, rows, block_len)
    depth1 = -(-3 * fields // 128) * 128
    weight1 = wide_weight(conv1_weight, depth1)
    weight2 = wide_weight(conv2_weight, 3 * hid)
    bias1 = jnp.concatenate([conv1_bias, conv1_bias])[:, None]
    bias2 = jnp.concatenate([conv2_bias, conv2_bias])[:, None]
    halo = exchange(regridded, low, high, plan, tables)
    hidden, low, high = conv(regridded, *halo, weight1, bias1, False)
    halo = exchange(hidden, low, high, plan, tables)
    return conv(hidden, *halo, weight2, bias2, True)


def solution(mesh):
    return jax.shard_map(
        local,
        mesh=mesh,
        in_specs=(
            P(None, AXES),
            P(AXES, None, None, None),
            P(AXES, None),
            P(AXES, None),
            P(),
            P(),
            P(),
            P(),
            P(),
        ),
        out_specs=P(None, None, "band", "tile"),
        check_vma=False,
    )
```

```python
import functools

import jax
import jax.numpy as jnp
import numpy as np
from jax import lax
from jax.experimental import pallas as pl
from jax.experimental.pallas import tpu as pltpu
from jax.sharding import PartitionSpec as P

BF = jnp.bfloat16
F32 = jnp.float32
AXES = ("band", "tile")
VMEM_LIMIT = 56 * 1024 * 1024


def regrid_kernel(pos_ref, src_ref, w_ref, out_ref, *, blocks, top, length):
    step = pl.program_id(0)
    for s in range(blocks):
        lhs = src_ref[:, s * length : (s + 1) * length]
        rhs = jnp.concatenate([w_ref[s, k] for k in range(top)], axis=1)
        val = jnp.dot(lhs, rhs, preferred_element_type=F32).astype(BF)
        for k in range(top):
            where = pos_ref[(step * blocks + s) * top + k]
            out_ref[where] = val[:, k * length : (k + 1) * length]


def regrid(source, weights, position, slots):
    fields = source.shape[0]
    count, top, length = weights.shape[0], weights.shape[1], weights.shape[2]
    blocks = 8
    return pl.pallas_call(
        functools.partial(regrid_kernel, blocks=blocks, top=top, length=length),
        grid_spec=pltpu.PrefetchScalarGridSpec(
            num_scalar_prefetch=1,
            grid=(count // blocks,),
            in_specs=[
                pl.BlockSpec((fields, blocks * length), lambda i, p: (0, i)),
                pl.BlockSpec((blocks, top, length, length), lambda i, p: (i, 0, 0, 0)),
            ],
            out_specs=pl.BlockSpec((slots, fields, length), lambda i, p: (0, 0, 0)),
        ),
        out_shape=jax.ShapeDtypeStruct((slots, fields, length), BF),
        compiler_params=pltpu.CompilerParams(vmem_limit_bytes=VMEM_LIMIT),
        cost_estimate=pl.CostEstimate(
            flops=2 * count * top * length * length * fields, bytes_accessed=17_000_000, transcendentals=0
        ),
    )(position, source, weights)


def edge_columns(piece, lane, at, low, high):
    cols = piece.shape[1]
    here = lane == at
    low = jnp.where(here, pltpu.roll(piece, at, 1) if at else piece, low)
    high = jnp.where(here, pltpu.roll(piece, (at + 1) % cols, 1), high)
    return low, high


def place_kernel(slot_ref, in_ref, out_ref, low_ref, high_ref, acc_ref, *, chunk):
    step = pl.program_id(0)

    @pl.when(step == 0)
    def _():
        acc_ref[...] = jnp.zeros_like(acc_ref)

    def body(i, carry):
        where = slot_ref[step * chunk + i]
        acc_ref[where] += in_ref[i].astype(F32)
        return carry

    lax.fori_loop(0, chunk, body, 0, unroll=8)

    @pl.when(step == pl.num_programs(0) - 1)
    def _():
        count, chans, cols = out_ref.shape
        lane = lax.broadcasted_iota(jnp.int32, (chans, cols), 1)
        for half in range(2):
            low = high = jnp.zeros((chans, cols), F32)
            for at in range(min(cols, count - half * cols)):
                piece = acc_ref[half * cols + at]
                out_ref[half * cols + at] = piece.astype(BF)
                low, high = edge_columns(piece, lane, at, low, high)
            low_ref[:, half * cols : (half + 1) * cols] = low.astype(BF)
            high_ref[:, half * cols : (half + 1) * cols] = high.astype(BF)


def place(arrived, slots, count):
    items, fields, length = arrived.shape
    chunk = 96
    return pl.pallas_call(
        functools.partial(place_kernel, chunk=chunk),
        grid_spec=pltpu.PrefetchScalarGridSpec(
            num_scalar_prefetch=1,
            grid=(items // chunk,),
            in_specs=[pl.BlockSpec((chunk, fields, length), lambda i, p: (i, 0, 0))],
            out_specs=[
                pl.BlockSpec((count, fields, length), lambda i, p: (0, 0, 0)),
                pl.BlockSpec((fields, 2 * length), lambda i, p: (0, 0)),
                pl.BlockSpec((fields, 2 * length), lambda i, p: (0, 0)),
            ],
            scratch_shapes=[pltpu.VMEM((count + 1, fields, length), F32)],
        ),
        out_shape=[
            jax.ShapeDtypeStruct((count, fields, length), BF),
            jax.ShapeDtypeStruct((fields, 2 * length), BF),
            jax.ShapeDtypeStruct((fields, 2 * length), BF),
        ],
        compiler_params=pltpu.CompilerParams(vmem_limit_bytes=VMEM_LIMIT),
    )(slots, arrived)


def gelu(v):
    return 0.5 * v * (1.0 + lax.erf(v * np.float32(1.0 / np.sqrt(2.0))))


def conv_kernel(w_ref, b_ref, x_ref, top_ref, bot_ref, l_ref, r_ref, *refs, last):
    if not last:
        edge_ref, refs = refs[0], refs[1:]
    if last:
        o_ref, p_ref, s_ref = refs
    else:
        o_ref, low_ref, high_ref, p_ref = refs
    faces, rows, chans, cols = x_ref.shape
    depth = p_ref.shape[1]
    hid = b_ref.shape[0] // 2
    pitch = hid + 8
    step = pl.program_id(0)
    lane = lax.broadcasted_iota(jnp.int32, (chans, cols), 1)
    spare = depth - 3 * chans
    span = rows + 2
    group = pl.ds(pl.multiple_of((step // 3) * cols, cols), cols)
    back = lax.rem(cols - lax.rem(step, 3) * (faces * span), cols)
    kind = F32 if chans % 16 else BF
    left = pltpu.roll(l_ref[:, group].astype(F32), back, 1).astype(kind)
    right = pltpu.roll(r_ref[:, group].astype(F32), back, 1).astype(kind)
    for f in range(faces):
        for r in range(span):
            row = top_ref[f] if r == 0 else bot_ref[f] if r == rows + 1 else x_ref[f, r - 1]
            mid = row.astype(kind)
            at = f * span + r
            lo = jnp.where(lane == 0, left[:, at : at + 1], pltpu.roll(mid, 1, 1))
            hi = jnp.where(lane == cols - 1, right[:, at : at + 1], pltpu.roll(mid, cols - 1, 1))
            parts = [lo, mid, hi]
            if spare:
                parts.append(jnp.zeros((spare, cols), F32))
            p_ref[r, :, f * cols : (f + 1) * cols] = jnp.concatenate(parts, axis=0).astype(BF)
    bias = b_ref[...]
    edges = jnp.zeros((2 * hid, 2 * cols), F32)
    for rp in range(rows // 2):
        patch = p_ref[2 * rp : 2 * rp + 4].reshape(4 * depth, faces * cols)
        acc = jnp.dot(w_ref[...], patch, preferred_element_type=F32) + bias
        acc = gelu(acc)
        if not last:
            acc = acc.astype(BF)
            edges += jnp.dot(acc, edge_ref[rp], preferred_element_type=F32)
        for d in range(2):
            for f in range(faces):
                piece = acc[d * hid : (d + 1) * hid, f * cols : (f + 1) * cols]
                if last:
                    s_ref[f, (2 * rp + d) * pitch : (2 * rp + d) * pitch + hid, :] = piece
                else:
                    o_ref[f, 2 * rp + d] = piece
    if last:
        for f in range(faces):
            for o in range(hid):
                o_ref[o, f] = s_ref[f, pl.ds(o, rows, stride=pitch), :].astype(BF)
    else:
        per = cols // (faces * rows)
        ahead = lax.rem(step, per) * (faces * rows)
        half = pl.ds(pl.multiple_of((step // per) * cols, cols), cols)
        fresh = lax.rem(step, per) == 0
        for i, ref in enumerate((low_ref, high_ref)):
            value = edges[:hid, i * cols : (i + 1) * cols] + pltpu.roll(edges[hid:, i * cols : (i + 1) * cols], 1, 1)
            value = pltpu.roll(value, ahead, 1).astype(BF)

            @pl.when(fresh)
            def _(ref=ref, value=value):
                ref[:, half] = value

            @pl.when(jnp.logical_not(fresh))
            def _(ref=ref, value=value):
                ref[:, half] += value


def edge_maps(faces, rows, cols):
    maps = np.zeros((rows // 2, faces * cols, 2 * cols), np.float32)
    for rp in range(rows // 2):
        for f in range(faces):
            maps[rp, f * cols, f * rows + 2 * rp] = 1
            maps[rp, f * cols + cols - 1, cols + f * rows + 2 * rp] = 1
    return jnp.asarray(maps, BF)


def conv(x, top, bottom, left, right, weight, bias, last):
    face_count, rows, chans, cols = x.shape
    depth = weight.shape[1] // 4
    hid = weight.shape[0] // 2
    faces = 2
    scratch = [pltpu.VMEM((rows + 2, depth, faces * cols), BF)]
    if last:
        out_shape = jax.ShapeDtypeStruct((hid, face_count, rows, cols), BF)
        out_spec = pl.BlockSpec((hid, faces, rows, cols), lambda i: (0, i, 0, 0))
        scratch.append(pltpu.VMEM((faces, rows * (hid + 8), cols), F32))
    else:
        out_shape = [jax.ShapeDtypeStruct((face_count, rows, hid, cols), BF)]
        out_shape += [jax.ShapeDtypeStruct((hid, 2 * cols), BF)] * 2
        out_spec = [pl.BlockSpec((faces, rows, hid, cols), lambda i: (i, 0, 0, 0))]
        out_spec += [pl.BlockSpec((hid, 2 * cols), lambda i: (0, 0))] * 2
    return pl.pallas_call(
        functools.partial(conv_kernel, last=last),
        grid=(face_count // faces,),
        in_specs=[
            pl.BlockSpec(weight.shape, lambda i: (0, 0)),
            pl.BlockSpec(bias.shape, lambda i: (0, 0)),
            pl.BlockSpec((faces, rows, chans, cols), lambda i: (i, 0, 0, 0)),
            pl.BlockSpec((faces, chans, cols), lambda i: (i, 0, 0)),
            pl.BlockSpec((faces, chans, cols), lambda i: (i, 0, 0)),
            pl.BlockSpec(left.shape, lambda i: (0, 0)),
            pl.BlockSpec(right.shape, lambda i: (0, 0)),
        ]
        + ([] if last else [pl.BlockSpec((rows // 2, faces * cols, 2 * cols), lambda i: (0, 0, 0))]),
        out_specs=out_spec,
        out_shape=out_shape,
        scratch_shapes=scratch,
        compiler_params=pltpu.CompilerParams(vmem_limit_bytes=VMEM_LIMIT),
    )(weight, bias, x, top, bottom, left, right, *([] if last else [edge_maps(faces, rows, cols)]))


def wide_weight(weight, depth):
    taps, hid, chans = weight.shape
    rows = weight.reshape(3, 3, hid, chans).transpose(2, 0, 1, 3).reshape(hid, 3, 3 * chans)
    rows = jnp.pad(rows, ((0, 0), (0, 0), (0, depth - 3 * chans)))
    first = jnp.pad(rows, ((0, 0), (0, 1), (0, 0)))
    second = jnp.pad(rows, ((0, 0), (1, 0), (0, 0)))
    return jnp.stack([first, second]).reshape(2 * hid, 4 * depth)


class Plan:
    def __init__(self, bands, tiles):
        self.bands, self.tiles = bands, tiles
        self.per = bands // tiles
        per, last = self.per, bands - 1
        rounds = per + 1
        count = bands * tiles
        self.pairs = [[] for _ in range(rounds)]
        self.sends = np.zeros((rounds, count), np.int32)
        self.row_from = np.full((count, per), 2, np.int32)
        self.col_round = np.full((count,), rounds, np.int32)
        corners = (tiles - 1, last * tiles)
        self.pairs[per] = [corners, corners[::-1]]

        def join(row_dev, col_dev, j):
            if row_dev in corners and col_dev in corners:
                self.sends[per, row_dev] = 1 if j == 0 else 2
                self.row_from[row_dev, j] = 1
                self.col_round[col_dev] = per
                return
            self.sends[j, row_dev] = 1
            if row_dev != col_dev:
                self.pairs[j] += [(row_dev, col_dev), (col_dev, row_dev)]
                self.row_from[row_dev, j] = 0
                self.col_round[col_dev] = j

        for j in range(per):
            for t in range(tiles):
                join(t, (per * t + j) * tiles, j)
                join(last * tiles + t, (per * t + j) * tiles + tiles - 1, j)
        for pairs in self.pairs:
            assert len({a for a, _ in pairs}) == len(pairs) == len({b for _, b in pairs})
        self.flip_row = [
            (b * tiles + t, b * tiles + tiles - 1 - t) for b in (0, last) for t in range(tiles)
        ]
        self.flip_col = [(b * tiles + t, (last - b) * tiles + t) for b in range(bands) for t in (0, tiles - 1)]


def lane18(f, p, span, width):
    return (f // 6) * width + (f % 6) * span + p


def fixed_maps(faces, rows, cols):
    span = rows + 2
    own = np.zeros((3 * cols, 2 * cols), np.float32)
    wrap = np.zeros((4 * cols, 2 * cols), np.float32)
    widen = np.zeros((2 * cols, 2 * cols), np.float32)
    ends = np.zeros((2, 2 * cols, 2 * cols), np.float32)
    corner = np.zeros((2, 4 * cols, cols), np.float32)
    unit_ends = np.zeros((2, 2 * cols, 4 * cols), np.float32)
    for f in range(faces):
        for r in range(rows):
            to = lane18(f, r + 1, span, cols)
            own[f * rows + r, to] = wrap[f * rows + r, to] = widen[f * rows + r, to] = 1
        for which, p in ((0, 0), (1, span - 1)):
            to = lane18(f, p, span, cols)
            own[2 * cols + 16 * which + f, to] = 1
            wrap[(2 + which) * cols + 2 * f, to] = 1
            for side in range(2):
                ends[side, which * cols + 2 * f + side, to] = 1
        for which, r in ((0, 0), (1, rows - 1)):
            for side in range(2):
                corner[which, side * 2 * cols + f * rows + r, 2 * f + side] = 1
        for which, p in ((0, 0), (1, span - 1)):
            for pair in range(2):
                to = pair * 2 * cols + lane18(f, p, span, cols)
                unit_ends[which, pair * cols + 2 * f + which, to] = 1
    back = np.eye(cols)[::-1].copy()
    return [jnp.asarray(m, BF) for m in (own, wrap, widen, ends, corner, unit_ends, back)]


def seam_tables(seam_table, plan, rows, cols):
    band, tile = lax.axis_index("band"), lax.axis_index("tile")
    me = band * plan.tiles + tile
    faces = seam_table.shape[0]
    span = rows + 2
    per, rounds = plan.per, plan.per + 1
    last_band, last_tile = plan.bands - 1, plan.tiles - 1
    static = np.concatenate(
        [
            plan.col_round[:, None],
            plan.row_from[:, :1],
            plan.row_from[:, -1:],
            plan.sends.T,
        ],
        axis=1,
    ).astype(np.int32)
    static = lax.dynamic_slice_in_dim(jnp.asarray(static), me, 1, 0)[0]
    row = jnp.where(band == 0, seam_table[:, 0], seam_table[:, 1])
    col = jnp.where(tile == 0, seam_table[:, 2], seam_table[:, 3])
    scalars = jnp.concatenate(
        [jnp.stack([band, tile]).astype(jnp.int32), static, row[:, 1], row[:, 0], row[:, 2], jnp.zeros((4,), jnp.int32)]
    )
    lanes = np.full((2, 2 * cols), -1, np.int32)
    for f in range(faces):
        for p in range(span):
            lanes[:, lane18(f, p, span, cols)] = f, p
    face, place = lanes
    line_in = np.concatenate([np.where(face >= 0, face + faces * side, -1) for side in range(4)])
    place_in = np.tile(place, 4)
    col_line = col[:, 1] * faces + col[:, 0]
    hot = jnp.asarray(face[:, None] == np.arange(faces)[None, :])
    want = jnp.sum(jnp.where(hot, col_line[None, :], 0), axis=1)
    turned = jnp.sum(jnp.where(hot, col[:, 2][None, :], 0), axis=1)
    pick = (jnp.asarray(line_in)[:, None] == want[None, :]) & jnp.asarray(
        (place_in[:, None] == place[None, :]) & (face >= 0)[None, :]
    )
    corner = ((band == 0) & jnp.asarray(place == 0)) | ((band == last_band) & jnp.asarray(place == span - 1))
    same_face = (face[:, None] == face[None, :]) & (face >= 0)[None, :]
    keep = jnp.asarray(same_face & (place[:, None] == place[None, :])) & (turned == 0)[None, :]
    flip = jnp.asarray(same_face & (place[:, None] == span - 1 - place[None, :])) & (turned == 1)[None, :]
    join = jnp.concatenate([keep, flip]) & jnp.logical_not(corner)[None, :]
    at = np.arange(cols)
    end_face, end_side = np.where(at < 2 * faces, at // 2, -1), at % 2
    end_turned = jnp.sum(jnp.where(jnp.asarray(end_face[:, None] == np.arange(faces)[None, :]), row[:, 2][None, :], 0), axis=1)
    outer = ((tile == 0) & jnp.asarray(end_side == 0)) | ((tile == last_tile) & jnp.asarray(end_side == 1))
    same_end = (end_face[:, None] == end_face[None, :]) & (end_face >= 0)[None, :]
    keep_end = jnp.asarray(same_end & (end_side[:, None] == end_side[None, :])) & (end_turned == 0)[None, :]
    flip_end = jnp.asarray(same_end & (end_side[:, None] != end_side[None, :])) & (end_turned == 1)[None, :]
    join_end = jnp.concatenate([keep_end, flip_end]) & jnp.logical_not(outer)[None, :]
    return scalars, pick.astype(BF), join.astype(BF), join_end.astype(BF), fixed_maps(faces, rows, cols)


BAND, TILE, COL_ROUND, FIRST_FROM, LAST_FROM, SENDS = 0, 1, 2, 3, 4, 5


def whole(kernel, out_shape, scratch, scalars, *args):
    return pl.pallas_call(
        kernel,
        in_specs=[pl.BlockSpec(memory_space=pltpu.SMEM)] + [pl.BlockSpec(memory_space=pltpu.VMEM)] * len(args),
        out_specs=[pl.BlockSpec(memory_space=pltpu.VMEM)] * len(out_shape),
        out_shape=[jax.ShapeDtypeStruct(s, BF) for s in out_shape],
        scratch_shapes=scratch,
        compiler_params=pltpu.CompilerParams(vmem_limit_bytes=VMEM_LIMIT),
    )(scalars, *args)


def pick2(cond, a, b):
    return lax.select_n(cond, b, a)


def side_by_side(*parts):
    return jnp.concatenate(parts, axis=1)


def move(x, matrix):
    return jnp.dot(x, matrix, preferred_element_type=F32)


def rows_kernel(first_ref, last_ref, left_ref, right_ref, corner_ref, up_ref, down_ref):
    faces = first_ref.shape[0]
    both = side_by_side(left_ref[...], right_ref[...])
    for which, (src, out) in enumerate(((first_ref, up_ref), (last_ref, down_ref))):
        for f in range(faces):
            out[f] = src[f, 0]
        out[faces] = move(both, corner_ref[which]).astype(BF)


def rows_call(x, left, right, corner):
    faces, rows, chans, cols = x.shape
    full = lambda a: pl.BlockSpec(a.shape, lambda i: (0,) * a.ndim)
    out = jax.ShapeDtypeStruct((faces + 1, chans, cols), BF)
    return pl.pallas_call(
        rows_kernel,
        grid=(1,),
        in_specs=[
            pl.BlockSpec((faces, 1, chans, cols), lambda i: (0, 0, 0, 0)),
            pl.BlockSpec((faces, 1, chans, cols), lambda i: (0, rows - 1, 0, 0)),
            full(left),
            full(right),
            full(corner),
        ],
        out_specs=[pl.BlockSpec(out.shape, lambda i: (0, 0, 0))] * 2,
        out_shape=[out] * 2,
        compiler_params=pltpu.CompilerParams(vmem_limit_bytes=VMEM_LIMIT),
    )(x, x, left, right, corner)


def lines_kernel(s_ref, up_ref, down_ref, top_ref, bot_ref, low_ref, high_ref, left_ref, right_ref, own_ref, wrap_ref, ue_ref, *outs, bands, rows):
    messages, both_ref, cl_ref = outs[:-2], outs[-2], outs[-1]
    per = len(messages)
    faces, (chans, cols) = up_ref.shape[0] - 1, up_ref.shape[1:]
    span = rows + 2
    first_band, first_tile = s_ref[BAND] == 0, s_ref[TILE] == 0
    lane = lax.broadcasted_iota(jnp.int32, (chans, cols), 1)
    top_edge = jnp.zeros((chans, cols), F32)
    for which, ref in enumerate((top_ref, bot_ref)):
        for f in range(faces):
            at = 16 * which + f
            row = ref[f].astype(F32)
            value = pltpu.roll(row, pick2(first_tile, jnp.int32(at), jnp.int32(at + 1)), 1)
            top_edge = jnp.where(lane == at, value, top_edge)
    mine = pick2(first_tile, low_ref[...], high_ref[...])
    theirs = pick2(first_tile, left_ref[...], right_ref[...])
    turn = pick2(first_tile, jnp.int32(0), jnp.int32(cols - 1))
    tc = pltpu.roll(top_ref[faces].astype(F32), turn, 1).astype(BF)
    bc = pltpu.roll(bot_ref[faces].astype(F32), turn, 1).astype(BF)
    own = move(side_by_side(mine, top_edge.astype(BF)), own_ref[...]).astype(BF)
    wrap = move(side_by_side(theirs, tc, bc), wrap_ref[...]).astype(BF)
    cl_ref[...] = side_by_side(pick2(first_tile, own, wrap), pick2(first_tile, wrap, own))
    on_row = jnp.logical_or(first_band, s_ref[BAND] == bands - 1)
    both_ref[:, : 4 * cols] = cl_ref[...]
    both_ref[:, 4 * cols :] = jnp.zeros((chans, 4 * cols), BF)
    for m in range(per):

        @pl.when(s_ref[SENDS + m] == 0)
        def _(m=m):
            messages[m][...] = cl_ref[...]

    @pl.when(on_row)
    def _():
        ends = side_by_side(pick2(first_band, up_ref[faces], bot_ref[faces]), pick2(first_band, top_ref[faces], down_ref[faces]))
        for g in range(4):
            pieces = [jnp.zeros((chans, cols), F32) for _ in range(per)]
            for i in range(6):
                pair, f = divmod(6 * g + i, faces)
                line = pick2(first_band, up_ref[f], bot_ref[f]) if pair == 0 else pick2(first_band, top_ref[f], down_ref[f])
                line = line.astype(F32)
                for j in range(per):
                    low = i * span + (1 if j == 0 else 0)
                    high = i * span + span - (1 if j == per - 1 else 0)
                    value = pltpu.roll(line, (i * span + 1 - rows * j) % cols, 1)
                    pieces[j] = jnp.where((lane >= low) & (lane < high), value, pieces[j])
            where = slice(g * cols, (g + 1) * cols)
            for j in (0, per - 1):
                pieces[j] = pieces[j] + move(ends, ue_ref[0 if j == 0 else 1, :, where])
            for j in range(per):

                @pl.when(s_ref[SENDS + j] == 1)
                def _(j=j, piece=pieces[j]):
                    messages[j][:, where] = piece.astype(BF)

            second = slice((4 + g) * cols, (5 + g) * cols)
            for code, j in ((1, 0), (2, per - 1)):

                @pl.when(s_ref[SENDS + per] == code)
                def _(piece=pieces[j]):
                    both_ref[:, second] = piece.astype(BF)


def seams_kernel(s_ref, *refs, rounds, rows, bands):
    got, refs = refs[:rounds], refs[rounds:]
    first_msg, last_msg, cl_ref, up_ref, down_ref, top_ref, bot_ref, pick_ref, srow_ref, scol_ref = refs[:10]
    rows_ref, unit0_ref, unit7_ref, other_ref, corner_ref = refs[10:]
    faces, (chans, cols) = up_ref.shape[0] - 1, up_ref.shape[1:]
    per = rounds - 1
    span = rows + 2
    first_band = s_ref[BAND] == 0
    lane = lax.broadcasted_iota(jnp.int32, (chans, cols), 1)
    for r in range(rounds):

        @pl.when(s_ref[COL_ROUND] == r)
        def _(r=r):
            other_ref[...] = got[r][:, got[r].shape[1] - 4 * cols :]

    @pl.when((s_ref[COL_ROUND] == rounds) & first_band)
    def _():
        other_ref[...] = first_msg[...]

    @pl.when((s_ref[COL_ROUND] == rounds) & jnp.logical_not(first_band))
    def _():
        other_ref[...] = last_msg[...]

    scol_ref[...] = move(side_by_side(other_ref[...], cl_ref[...]), pick_ref[...]).astype(BF)

    on_row = jnp.logical_or(first_band, s_ref[BAND] == bands - 1)
    table = SENDS + rounds

    @pl.when(on_row)
    def _():
        for code, to, normal in ((FIRST_FROM, unit0_ref, got[0]), (LAST_FROM, unit7_ref, got[per - 1])):
            for value, src in enumerate((normal, got[per], cl_ref)):

                @pl.when(s_ref[code] == value)
                def _(to=to, src=src):
                    to[...] = src[:, : 4 * cols]

        for f in range(faces + 1):
            rows_ref[f] = pick2(first_band, up_ref[f], bot_ref[f])
            rows_ref[faces + 1 + f] = pick2(first_band, top_ref[f], down_ref[f])
        units = [unit0_ref, *got[1 : per - 1], unit7_ref]
        corner_ref[...] = jnp.zeros_like(corner_ref)
        for f in range(faces):
            side, face = s_ref[table + f], s_ref[table + faces + f]

            @pl.when(side < 2)
            def _(f=f, side=side, face=face):
                srow_ref[f] = rows_ref[side * (faces + 1) + face]
                ends = rows_ref[side * (faces + 1) + faces].astype(F32)
                ends = pltpu.roll(ends, lax.rem(2 * f + 2 * cols - 2 * face, cols), 1)
                corner_ref[...] = jnp.where((lane == 2 * f) | (lane == 2 * f + 1), ends, corner_ref[...])

            @pl.when(side >= 2)
            def _(f=f, side=side, face=face):
                group = pl.ds(pl.multiple_of(((side - 2) * 2 + face // 6) * cols, cols), cols)
                q = lax.rem(face, 6) * span
                line = jnp.zeros((chans, cols), F32)
                ends = corner_ref[...]
                for j in range(per):
                    value = units[j][:, group].astype(F32)
                    line = jnp.where(lane // rows == j, pltpu.roll(value, lax.rem(rows * j + 2 * cols - 1 - q, cols), 1), line)
                    if j == 0:
                        ends = jnp.where(lane == 2 * f, pltpu.roll(value, lax.rem(2 * f + 2 * cols - q, cols), 1), ends)
                    if j == per - 1:
                        shift = lax.rem(2 * f + 1 + 2 * cols - q - (span - 1), cols)
                        ends = jnp.where(lane == 2 * f + 1, pltpu.roll(value, shift, 1), ends)
                srow_ref[f] = line.astype(BF)
                corner_ref[...] = ends

        srow_ref[faces] = corner_ref[...].astype(BF)

    @pl.when(jnp.logical_not(on_row))
    def _():
        srow_ref[...] = jnp.zeros_like(srow_ref)


def halo_kernel(s_ref, srow_ref, rrow_ref, scol_ref, rcol_ref, top_ref, bot_ref, left_ref, right_ref, join_ref, joinend_ref, back_ref, widen_ref, ends_ref, t_out, b_out, l_out, r_out, *, bands, tiles, rounds):
    faces, (chans, cols) = top_ref.shape[0] - 1, top_ref.shape[1:]
    first_band, last_band = s_ref[BAND] == 0, s_ref[BAND] == bands - 1
    first_tile, last_tile = s_ref[TILE] == 0, s_ref[TILE] == tiles - 1
    table = SENDS + rounds + 2 * faces
    for cond, out, ref in ((first_band, t_out, top_ref), (last_band, b_out, bot_ref)):

        @pl.when(cond)
        def _(out=out):
            for f in range(faces):
                turned = move(rrow_ref[f], back_ref[...]).astype(BF)
                out[f] = pick2(s_ref[table + f] == 1, turned, srow_ref[f])

        @pl.when(jnp.logical_not(cond))
        def _(out=out, ref=ref):
            for f in range(faces):
                out[f] = ref[f]

    ends = move(side_by_side(srow_ref[faces], rrow_ref[faces]), joinend_ref[...]).astype(BF)
    top_end = pick2(first_band, ends, top_ref[faces])
    bot_end = pick2(last_band, ends, bot_ref[faces])
    none = jnp.zeros_like(top_end)
    seam = move(side_by_side(scol_ref[...], rcol_ref[...]), join_ref[...])
    for side, (at_edge, src, out) in enumerate(((first_tile, left_ref, l_out), (last_tile, right_ref, r_out))):
        use_top = jnp.logical_or(first_band, jnp.logical_not(at_edge))
        use_bot = jnp.logical_or(last_band, jnp.logical_not(at_edge))
        both = side_by_side(pick2(use_top, top_end, none), pick2(use_bot, bot_end, none))
        base = pick2(at_edge, seam, move(src[...], widen_ref[...]))
        out[...] = (base + move(both, ends_ref[side])).astype(BF)


def exchange(x, low, high, plan, tables):
    scalars, pick, join, join_end, (own, wrap, widen, ends, corner, unit_ends, back) = tables
    faces, rows, chans, cols = x.shape
    bands, tiles = plan.bands, plan.tiles
    rounds = len(plan.pairs)
    across = [(i, (i + 1) % tiles) for i in range(tiles)]
    left = lax.ppermute(high, "tile", across)
    right = lax.ppermute(low, "tile", [(j, i) for i, j in across])
    up, down = rows_call(x, left, right, corner)
    around = [(i, (i + 1) % bands) for i in range(bands)]
    top = lax.ppermute(down, "band", around)
    bottom = lax.ppermute(up, "band", [(j, i) for i, j in around])
    outs = whole(
        functools.partial(lines_kernel, bands=bands, rows=rows),
        [(chans, 4 * cols)] * plan.per + [(chans, 8 * cols), (chans, 4 * cols)],
        [],
        scalars, up, down, top, bottom, low, high, left, right, own, wrap, unit_ends,
    )
    messages, col_lines = outs[:-1], outs[-1]
    got = [lax.ppermute(m, AXES, pairs) for m, pairs in zip(messages, plan.pairs)]
    line = (faces + 1, chans, cols)
    srow, scol = whole(
        functools.partial(seams_kernel, rounds=rounds, rows=rows, bands=bands),
        [line, (chans, 2 * cols)],
        [
            pltpu.VMEM((2 * (faces + 1), chans, cols), BF),
            pltpu.VMEM((chans, 4 * cols), BF),
            pltpu.VMEM((chans, 4 * cols), BF),
            pltpu.VMEM((chans, 4 * cols), BF),
            pltpu.VMEM((chans, cols), F32),
        ],
        scalars, *got, messages[0], messages[plan.per - 1], col_lines, up, down, top, bottom, pick,
    )
    rrow = lax.ppermute(srow, AXES, plan.flip_row)
    rcol = lax.ppermute(scol, AXES, plan.flip_col)
    rim = (faces, chans, cols)
    return whole(
        functools.partial(halo_kernel, bands=bands, tiles=tiles, rounds=rounds),
        [rim, rim, (chans, 2 * cols), (chans, 2 * cols)],
        [],
        scalars, srow, rrow, scol, rcol, top, bottom, left, right, join, join_end, back, widen, ends,
    )


def local(
    source,
    regrid_weights,
    dest_group,
    dest_block,
    seam_table,
    conv1_weight,
    conv1_bias,
    conv2_weight,
    conv2_bias,
):
    bands, tiles = lax.axis_size("band"), lax.axis_size("tile")
    devices = bands * tiles
    src_count, top_count, block_len = regrid_weights.shape[:3]
    capacity = 3 * src_count * top_count // devices
    rows = block_len * tiles // bands
    faces = seam_table.shape[0]
    slots_dev = faces * rows
    fields = source.shape[0]
    hid = conv1_weight.shape[1]
    items = src_count * top_count
    total = devices * capacity

    target = dest_group.reshape(items)
    order = jnp.arange(items)
    same = (target[:, None] == target[None, :]) & (order[None, :] < order[:, None])
    position = target * capacity + jnp.sum(same.astype(jnp.int32), axis=1)
    base = 1 << slots_dev.bit_length()
    codes = lax.all_gather(target * base + dest_block.reshape(items), AXES)
    mine = codes // base == lax.axis_index(AXES)
    earlier = jnp.asarray(np.triu(np.ones((items, items), np.float32), 1), BF)
    rank = jnp.dot(mine.astype(BF), earlier, preferred_element_type=F32).astype(jnp.int32)
    hit = mine[:, None, :] & (rank[:, None, :] == jnp.arange(capacity)[None, :, None])
    slots = slots_dev + jnp.sum(jnp.where(hit, (codes % base - slots_dev)[:, None, :], 0), axis=2)
    outgoing = regrid(source, regrid_weights, position, total)
    arrived = lax.all_to_all(
        outgoing.reshape(devices, capacity, fields, block_len), AXES, split_axis=0, concat_axis=0, tiled=True
    )
    regridded, low, high = place(arrived.reshape(total, fields, block_len), slots.reshape(total), slots_dev)
    regridded = regridded.reshape(faces, rows, fields, block_len)

    plan = Plan(bands, tiles)
    tables = seam_tables(seam_table, plan, rows, block_len)
    depth1 = -(-3 * fields // 128) * 128
    weight1 = wide_weight(conv1_weight, depth1)
    weight2 = wide_weight(conv2_weight, 3 * hid)
    bias1 = jnp.concatenate([conv1_bias, conv1_bias])[:, None]
    bias2 = jnp.concatenate([conv2_bias, conv2_bias])[:, None]
    halo = exchange(regridded, low, high, plan, tables)
    hidden, low, high = conv(regridded, *halo, weight1, bias1, False)
    halo = exchange(hidden, low, high, plan, tables)
    return conv(hidden, *halo, weight2, bias2, True)


def solution(mesh):
    return jax.shard_map(
        local,
        mesh=mesh,
        in_specs=(
            P(None, AXES),
            P(AXES, None, None, None),
            P(AXES, None),
            P(AXES, None),
            P(),
            P(),
            P(),
            P(),
            P(),
        ),
        out_specs=P(None, None, "band", "tile"),
        check_vma=False,
    )
```

```python
import functools

import jax
import jax.numpy as jnp
import numpy as np
from jax import lax
from jax.experimental import pallas as pl
from jax.experimental.pallas import tpu as pltpu
from jax.sharding import PartitionSpec as P

BF = jnp.bfloat16
F32 = jnp.float32
AXES = ("band", "tile")
VMEM_LIMIT = 56 * 1024 * 1024


def regrid_kernel(pos_ref, src_ref, w_ref, out_ref, *, blocks, top, length):
    step = pl.program_id(0)
    for s in range(blocks):
        lhs = src_ref[:, s * length : (s + 1) * length]
        rhs = jnp.concatenate([w_ref[s, k] for k in range(top)], axis=1)
        val = jnp.dot(lhs, rhs, preferred_element_type=F32).astype(BF)
        for k in range(top):
            where = pos_ref[(step * blocks + s) * top + k]
            out_ref[where] = val[:, k * length : (k + 1) * length]


def regrid(source, weights, position, slots):
    fields = source.shape[0]
    count, top, length = weights.shape[0], weights.shape[1], weights.shape[2]
    blocks = 8
    return pl.pallas_call(
        functools.partial(regrid_kernel, blocks=blocks, top=top, length=length),
        grid_spec=pltpu.PrefetchScalarGridSpec(
            num_scalar_prefetch=1,
            grid=(count // blocks,),
            in_specs=[
                pl.BlockSpec((fields, blocks * length), lambda i, p: (0, i)),
                pl.BlockSpec((blocks, top, length, length), lambda i, p: (i, 0, 0, 0)),
            ],
            out_specs=pl.BlockSpec((slots, fields, length), lambda i, p: (0, 0, 0)),
        ),
        out_shape=jax.ShapeDtypeStruct((slots, fields, length), BF),
        compiler_params=pltpu.CompilerParams(vmem_limit_bytes=VMEM_LIMIT),
        cost_estimate=pl.CostEstimate(
            flops=2 * count * top * length * length * fields, bytes_accessed=17_000_000, transcendentals=0
        ),
    )(position, source, weights)


def edge_columns(piece, lane, at, low, high):
    cols = piece.shape[1]
    here = lane == at
    low = jnp.where(here, pltpu.roll(piece, at, 1) if at else piece, low)
    high = jnp.where(here, pltpu.roll(piece, (at + 1) % cols, 1), high)
    return low, high


def place_kernel(slot_ref, in_ref, out_ref, low_ref, high_ref, acc_ref, acc2_ref, *, chunk):
    step = pl.program_id(0)

    @pl.when(step == 0)
    def _():
        acc_ref[...] = jnp.zeros_like(acc_ref)
        acc2_ref[...] = jnp.zeros_like(acc2_ref)

    def body(i, carry):
        for j, ref in ((2 * i, acc_ref), (2 * i + 1, acc2_ref)):
            where = slot_ref[step * chunk + j]
            ref[where] += in_ref[j].astype(F32)
        return carry

    lax.fori_loop(0, chunk // 2, body, 0, unroll=8)

    @pl.when(step == pl.num_programs(0) - 1)
    def _():
        count, chans, cols = out_ref.shape
        lane = lax.broadcasted_iota(jnp.int32, (chans, cols), 1)
        for half in range(2):
            low = high = jnp.zeros((chans, cols), F32)
            for at in range(min(cols, count - half * cols)):
                piece = acc_ref[half * cols + at] + acc2_ref[half * cols + at]
                out_ref[half * cols + at] = piece.astype(BF)
                low, high = edge_columns(piece, lane, at, low, high)
            low_ref[:, half * cols : (half + 1) * cols] = low.astype(BF)
            high_ref[:, half * cols : (half + 1) * cols] = high.astype(BF)


def place(arrived, slots, count):
    items, fields, length = arrived.shape
    chunk = 96
    return pl.pallas_call(
        functools.partial(place_kernel, chunk=chunk),
        grid_spec=pltpu.PrefetchScalarGridSpec(
            num_scalar_prefetch=1,
            grid=(items // chunk,),
            in_specs=[pl.BlockSpec((chunk, fields, length), lambda i, p: (i, 0, 0))],
            out_specs=[
                pl.BlockSpec((count, fields, length), lambda i, p: (0, 0, 0)),
                pl.BlockSpec((fields, 2 * length), lambda i, p: (0, 0)),
                pl.BlockSpec((fields, 2 * length), lambda i, p: (0, 0)),
            ],
            scratch_shapes=[pltpu.VMEM((count + 1, fields, length), F32)] * 2,
        ),
        out_shape=[
            jax.ShapeDtypeStruct((count, fields, length), BF),
            jax.ShapeDtypeStruct((fields, 2 * length), BF),
            jax.ShapeDtypeStruct((fields, 2 * length), BF),
        ],
        compiler_params=pltpu.CompilerParams(vmem_limit_bytes=VMEM_LIMIT),
    )(slots, arrived)


def gelu(v):
    return 0.5 * v * (1.0 + lax.erf(v * np.float32(1.0 / np.sqrt(2.0))))


def conv_kernel(w_ref, b_ref, x_ref, top_ref, bot_ref, l_ref, r_ref, *refs, last):
    if not last:
        edge_ref, refs = refs[0], refs[1:]
    if last:
        o_ref, p_ref, s_ref = refs
    else:
        o_ref, low_ref, high_ref, p_ref = refs
    faces, rows, chans, cols = x_ref.shape
    depth = p_ref.shape[1]
    hid = b_ref.shape[0] // 2
    pitch = hid + 8
    step = pl.program_id(0)
    lane = lax.broadcasted_iota(jnp.int32, (chans, cols), 1)
    spare = depth - 3 * chans
    span = rows + 2
    group = pl.ds(pl.multiple_of((step // 3) * cols, cols), cols)
    back = lax.rem(cols - lax.rem(step, 3) * (faces * span), cols)
    kind = F32 if chans % 16 else BF
    left = pltpu.roll(l_ref[:, group].astype(F32), back, 1).astype(kind)
    right = pltpu.roll(r_ref[:, group].astype(F32), back, 1).astype(kind)
    for f in range(faces):
        for r in range(span):
            row = top_ref[f] if r == 0 else bot_ref[f] if r == rows + 1 else x_ref[f, r - 1]
            mid = row.astype(kind)
            at = f * span + r
            lo = jnp.where(lane == 0, left[:, at : at + 1], pltpu.roll(mid, 1, 1))
            hi = jnp.where(lane == cols - 1, right[:, at : at + 1], pltpu.roll(mid, cols - 1, 1))
            parts = [lo, mid, hi]
            if spare:
                parts.append(jnp.zeros((spare, cols), F32))
            p_ref[r, :, f * cols : (f + 1) * cols] = jnp.concatenate(parts, axis=0).astype(BF)
    bias = b_ref[...]
    edges = jnp.zeros((2 * hid, 2 * cols), F32)
    for rp in range(rows // 2):
        patch = p_ref[2 * rp : 2 * rp + 4].reshape(4 * depth, faces * cols)
        acc = jnp.dot(w_ref[...], patch, preferred_element_type=F32) + bias
        acc = gelu(acc)
        if not last:
            acc = acc.astype(BF)
            edges += jnp.dot(acc, edge_ref[rp], preferred_element_type=F32)
        for d in range(2):
            for f in range(faces):
                piece = acc[d * hid : (d + 1) * hid, f * cols : (f + 1) * cols]
                if last:
                    s_ref[f, (2 * rp + d) * pitch : (2 * rp + d) * pitch + hid, :] = piece
                else:
                    o_ref[f, 2 * rp + d] = piece
    if last:
        for f in range(faces):
            for o in range(hid):
                o_ref[o, f] = s_ref[f, pl.ds(o, rows, stride=pitch), :].astype(BF)
    else:
        per = cols // (faces * rows)
        ahead = lax.rem(step, per) * (faces * rows)
        half = pl.ds(pl.multiple_of((step // per) * cols, cols), cols)
        fresh = lax.rem(step, per) == 0
        for i, ref in enumerate((low_ref, high_ref)):
            value = edges[:hid, i * cols : (i + 1) * cols] + pltpu.roll(edges[hid:, i * cols : (i + 1) * cols], 1, 1)
            value = pltpu.roll(value, ahead, 1).astype(BF)

            @pl.when(fresh)
            def _(ref=ref, value=value):
                ref[:, half] = value

            @pl.when(jnp.logical_not(fresh))
            def _(ref=ref, value=value):
                ref[:, half] += value


def edge_maps(faces, rows, cols):
    maps = np.zeros((rows // 2, faces * cols, 2 * cols), np.float32)
    for rp in range(rows // 2):
        for f in range(faces):
            maps[rp, f * cols, f * rows + 2 * rp] = 1
            maps[rp, f * cols + cols - 1, cols + f * rows + 2 * rp] = 1
    return jnp.asarray(maps, BF)


def conv(x, top, bottom, left, right, weight, bias, last):
    face_count, rows, chans, cols = x.shape
    depth = weight.shape[1] // 4
    hid = weight.shape[0] // 2
    faces = 2
    scratch = [pltpu.VMEM((rows + 2, depth, faces * cols), BF)]
    if last:
        out_shape = jax.ShapeDtypeStruct((hid, face_count, rows, cols), BF)
        out_spec = pl.BlockSpec((hid, faces, rows, cols), lambda i: (0, i, 0, 0))
        scratch.append(pltpu.VMEM((faces, rows * (hid + 8), cols), F32))
    else:
        out_shape = [jax.ShapeDtypeStruct((face_count, rows, hid, cols), BF)]
        out_shape += [jax.ShapeDtypeStruct((hid, 2 * cols), BF)] * 2
        out_spec = [pl.BlockSpec((faces, rows, hid, cols), lambda i: (i, 0, 0, 0))]
        out_spec += [pl.BlockSpec((hid, 2 * cols), lambda i: (0, 0))] * 2
    return pl.pallas_call(
        functools.partial(conv_kernel, last=last),
        grid=(face_count // faces,),
        in_specs=[
            pl.BlockSpec(weight.shape, lambda i: (0, 0)),
            pl.BlockSpec(bias.shape, lambda i: (0, 0)),
            pl.BlockSpec((faces, rows, chans, cols), lambda i: (i, 0, 0, 0)),
            pl.BlockSpec((faces, chans, cols), lambda i: (i, 0, 0)),
            pl.BlockSpec((faces, chans, cols), lambda i: (i, 0, 0)),
            pl.BlockSpec(left.shape, lambda i: (0, 0)),
            pl.BlockSpec(right.shape, lambda i: (0, 0)),
        ]
        + ([] if last else [pl.BlockSpec((rows // 2, faces * cols, 2 * cols), lambda i: (0, 0, 0))]),
        out_specs=out_spec,
        out_shape=out_shape,
        scratch_shapes=scratch,
        compiler_params=pltpu.CompilerParams(vmem_limit_bytes=VMEM_LIMIT),
    )(weight, bias, x, top, bottom, left, right, *([] if last else [edge_maps(faces, rows, cols)]))


def wide_weight(weight, depth):
    taps, hid, chans = weight.shape
    rows = weight.reshape(3, 3, hid, chans).transpose(2, 0, 1, 3).reshape(hid, 3, 3 * chans)
    rows = jnp.pad(rows, ((0, 0), (0, 0), (0, depth - 3 * chans)))
    first = jnp.pad(rows, ((0, 0), (0, 1), (0, 0)))
    second = jnp.pad(rows, ((0, 0), (1, 0), (0, 0)))
    return jnp.stack([first, second]).reshape(2 * hid, 4 * depth)


class Plan:
    def __init__(self, bands, tiles):
        self.bands, self.tiles = bands, tiles
        self.per = bands // tiles
        per, last = self.per, bands - 1
        rounds = per + 1
        count = bands * tiles
        self.pairs = [[] for _ in range(rounds)]
        self.sends = np.zeros((rounds, count), np.int32)
        self.row_from = np.full((count, per), 2, np.int32)
        self.col_round = np.full((count,), rounds, np.int32)
        corners = (tiles - 1, last * tiles)
        self.pairs[per] = [corners, corners[::-1]]

        def join(row_dev, col_dev, j):
            if row_dev in corners and col_dev in corners:
                self.sends[per, row_dev] = 1 if j == 0 else 2
                self.row_from[row_dev, j] = 1
                self.col_round[col_dev] = per
                return
            self.sends[j, row_dev] = 1
            if row_dev != col_dev:
                self.pairs[j] += [(row_dev, col_dev), (col_dev, row_dev)]
                self.row_from[row_dev, j] = 0
                self.col_round[col_dev] = j

        for j in range(per):
            for t in range(tiles):
                join(t, (per * t + j) * tiles, j)
                join(last * tiles + t, (per * t + j) * tiles + tiles - 1, j)
        for pairs in self.pairs:
            assert len({a for a, _ in pairs}) == len(pairs) == len({b for _, b in pairs})
        self.flip_row = [
            (b * tiles + t, b * tiles + tiles - 1 - t) for b in (0, last) for t in range(tiles)
        ]
        self.flip_col = [(b * tiles + t, (last - b) * tiles + t) for b in range(bands) for t in (0, tiles - 1)]


def lane18(f, p, span, width):
    return (f // 6) * width + (f % 6) * span + p


def fixed_maps(faces, rows, cols):
    span = rows + 2
    own = np.zeros((3 * cols, 2 * cols), np.float32)
    wrap = np.zeros((4 * cols, 2 * cols), np.float32)
    widen = np.zeros((2 * cols, 2 * cols), np.float32)
    ends = np.zeros((2, 2 * cols, 2 * cols), np.float32)
    corner = np.zeros((2, 4 * cols, cols), np.float32)
    unit_ends = np.zeros((2, 2 * cols, 4 * cols), np.float32)
    for f in range(faces):
        for r in range(rows):
            to = lane18(f, r + 1, span, cols)
            own[f * rows + r, to] = wrap[f * rows + r, to] = widen[f * rows + r, to] = 1
        for which, p in ((0, 0), (1, span - 1)):
            to = lane18(f, p, span, cols)
            own[2 * cols + 16 * which + f, to] = 1
            wrap[(2 + which) * cols + 2 * f, to] = 1
            for side in range(2):
                ends[side, which * cols + 2 * f + side, to] = 1
        for which, r in ((0, 0), (1, rows - 1)):
            for side in range(2):
                corner[which, side * 2 * cols + f * rows + r, 2 * f + side] = 1
        for which, p in ((0, 0), (1, span - 1)):
            for pair in range(2):
                to = pair * 2 * cols + lane18(f, p, span, cols)
                unit_ends[which, pair * cols + 2 * f + which, to] = 1
    back = np.eye(cols)[::-1].copy()
    return [jnp.asarray(m, BF) for m in (own, wrap, widen, ends, corner, unit_ends, back)]


def seam_tables(seam_table, plan, rows, cols):
    band, tile = lax.axis_index("band"), lax.axis_index("tile")
    me = band * plan.tiles + tile
    faces = seam_table.shape[0]
    span = rows + 2
    per, rounds = plan.per, plan.per + 1
    last_band, last_tile = plan.bands - 1, plan.tiles - 1
    static = np.concatenate(
        [
            plan.col_round[:, None],
            plan.row_from[:, :1],
            plan.row_from[:, -1:],
            plan.sends.T,
        ],
        axis=1,
    ).astype(np.int32)
    static = lax.dynamic_slice_in_dim(jnp.asarray(static), me, 1, 0)[0]
    row = jnp.where(band == 0, seam_table[:, 0], seam_table[:, 1])
    col = jnp.where(tile == 0, seam_table[:, 2], seam_table[:, 3])
    scalars = jnp.concatenate(
        [jnp.stack([band, tile]).astype(jnp.int32), static, row[:, 1], row[:, 0], row[:, 2], jnp.zeros((4,), jnp.int32)]
    )
    lanes = np.full((2, 2 * cols), -1, np.int32)
    for f in range(faces):
        for p in range(span):
            lanes[:, lane18(f, p, span, cols)] = f, p
    face, place = lanes
    line_in = np.concatenate([np.where(face >= 0, face + faces * side, -1) for side in range(4)])
    place_in = np.tile(place, 4)
    col_line = col[:, 1] * faces + col[:, 0]
    hot = jnp.asarray(face[:, None] == np.arange(faces)[None, :])
    want = jnp.sum(jnp.where(hot, col_line[None, :], 0), axis=1)
    turned = jnp.sum(jnp.where(hot, col[:, 2][None, :], 0), axis=1)
    pick = (jnp.asarray(line_in)[:, None] == want[None, :]) & jnp.asarray(
        (place_in[:, None] == place[None, :]) & (face >= 0)[None, :]
    )
    corner = ((band == 0) & jnp.asarray(place == 0)) | ((band == last_band) & jnp.asarray(place == span - 1))
    same_face = (face[:, None] == face[None, :]) & (face >= 0)[None, :]
    keep = jnp.asarray(same_face & (place[:, None] == place[None, :])) & (turned == 0)[None, :]
    flip = jnp.asarray(same_face & (place[:, None] == span - 1 - place[None, :])) & (turned == 1)[None, :]
    join = jnp.concatenate([keep, flip]) & jnp.logical_not(corner)[None, :]
    at = np.arange(cols)
    end_face, end_side = np.where(at < 2 * faces, at // 2, -1), at % 2
    end_turned = jnp.sum(jnp.where(jnp.asarray(end_face[:, None] == np.arange(faces)[None, :]), row[:, 2][None, :], 0), axis=1)
    outer = ((tile == 0) & jnp.asarray(end_side == 0)) | ((tile == last_tile) & jnp.asarray(end_side == 1))
    same_end = (end_face[:, None] == end_face[None, :]) & (end_face >= 0)[None, :]
    keep_end = jnp.asarray(same_end & (end_side[:, None] == end_side[None, :])) & (end_turned == 0)[None, :]
    flip_end = jnp.asarray(same_end & (end_side[:, None] != end_side[None, :])) & (end_turned == 1)[None, :]
    join_end = jnp.concatenate([keep_end, flip_end]) & jnp.logical_not(outer)[None, :]
    return scalars, pick.astype(BF), join.astype(BF), join_end.astype(BF), fixed_maps(faces, rows, cols)


BAND, TILE, COL_ROUND, FIRST_FROM, LAST_FROM, SENDS = 0, 1, 2, 3, 4, 5


def whole(kernel, out_shape, scratch, scalars, *args):
    return pl.pallas_call(
        kernel,
        in_specs=[pl.BlockSpec(memory_space=pltpu.SMEM)] + [pl.BlockSpec(memory_space=pltpu.VMEM)] * len(args),
        out_specs=[pl.BlockSpec(memory_space=pltpu.VMEM)] * len(out_shape),
        out_shape=[jax.ShapeDtypeStruct(s, BF) for s in out_shape],
        scratch_shapes=scratch,
        compiler_params=pltpu.CompilerParams(vmem_limit_bytes=VMEM_LIMIT),
    )(scalars, *args)


def pick2(cond, a, b):
    return lax.select_n(cond, b, a)


def side_by_side(*parts):
    return jnp.concatenate(parts, axis=1)


def move(x, matrix):
    return jnp.dot(x, matrix, preferred_element_type=F32)


def rows_kernel(first_ref, last_ref, left_ref, right_ref, corner_ref, up_ref, down_ref):
    faces = first_ref.shape[0]
    both = side_by_side(left_ref[...], right_ref[...])
    for which, (src, out) in enumerate(((first_ref, up_ref), (last_ref, down_ref))):
        for f in range(faces):
            out[f] = src[f, 0]
        out[faces] = move(both, corner_ref[which]).astype(BF)


def rows_call(x, left, right, corner):
    faces, rows, chans, cols = x.shape
    full = lambda a: pl.BlockSpec(a.shape, lambda i: (0,) * a.ndim)
    out = jax.ShapeDtypeStruct((faces + 1, chans, cols), BF)
    return pl.pallas_call(
        rows_kernel,
        grid=(1,),
        in_specs=[
            pl.BlockSpec((faces, 1, chans, cols), lambda i: (0, 0, 0, 0)),
            pl.BlockSpec((faces, 1, chans, cols), lambda i: (0, rows - 1, 0, 0)),
            full(left),
            full(right),
            full(corner),
        ],
        out_specs=[pl.BlockSpec(out.shape, lambda i: (0, 0, 0))] * 2,
        out_shape=[out] * 2,
        compiler_params=pltpu.CompilerParams(vmem_limit_bytes=VMEM_LIMIT),
    )(x, x, left, right, corner)


def lines_kernel(s_ref, up_ref, down_ref, top_ref, bot_ref, low_ref, high_ref, left_ref, right_ref, own_ref, wrap_ref, ue_ref, *outs, bands, rows):
    messages, both_ref, cl_ref = outs[:-2], outs[-2], outs[-1]
    per = len(messages)
    faces, (chans, cols) = up_ref.shape[0] - 1, up_ref.shape[1:]
    span = rows + 2
    kind = F32 if chans % 16 else BF
    first_band, first_tile = s_ref[BAND] == 0, s_ref[TILE] == 0
    lane = lax.broadcasted_iota(jnp.int32, (chans, cols), 1)
    top_edge = jnp.zeros((chans, cols), F32)
    for which, ref in enumerate((top_ref, bot_ref)):
        for f in range(faces):
            at = 16 * which + f
            row = ref[f].astype(F32)
            value = pltpu.roll(row, pick2(first_tile, jnp.int32(at), jnp.int32(at + 1)), 1)
            top_edge = jnp.where(lane == at, value, top_edge)
    mine = pick2(first_tile, low_ref[...], high_ref[...])
    theirs = pick2(first_tile, left_ref[...], right_ref[...])
    turn = pick2(first_tile, jnp.int32(0), jnp.int32(cols - 1))
    tc = pltpu.roll(top_ref[faces].astype(F32), turn, 1).astype(BF)
    bc = pltpu.roll(bot_ref[faces].astype(F32), turn, 1).astype(BF)
    own = move(side_by_side(mine, top_edge.astype(BF)), own_ref[...]).astype(BF)
    wrap = move(side_by_side(theirs, tc, bc), wrap_ref[...]).astype(BF)
    cl_ref[...] = side_by_side(pick2(first_tile, own, wrap), pick2(first_tile, wrap, own))
    on_row = jnp.logical_or(first_band, s_ref[BAND] == bands - 1)
    both_ref[:, : 4 * cols] = cl_ref[...]
    both_ref[:, 4 * cols :] = jnp.zeros((chans, 4 * cols), BF)
    for m in range(per):

        @pl.when(s_ref[SENDS + m] == 0)
        def _(m=m):
            messages[m][...] = cl_ref[...]

    @pl.when(on_row)
    def _():
        ends = side_by_side(pick2(first_band, up_ref[faces], bot_ref[faces]), pick2(first_band, top_ref[faces], down_ref[faces]))
        for g in range(4):
            pieces = [jnp.zeros((chans, cols), kind) for _ in range(per)]
            for i in range(6):
                pair, f = divmod(6 * g + i, faces)
                line = pick2(first_band, up_ref[f], bot_ref[f]) if pair == 0 else pick2(first_band, top_ref[f], down_ref[f])
                line = line.astype(kind)
                for j in range(per):
                    low = i * span + (1 if j == 0 else 0)
                    high = i * span + span - (1 if j == per - 1 else 0)
                    value = pltpu.roll(line, (i * span + 1 - rows * j) % cols, 1)
                    pieces[j] = jnp.where((lane >= low) & (lane < high), value, pieces[j])
            where = slice(g * cols, (g + 1) * cols)
            for j in (0, per - 1):
                pieces[j] = pieces[j] + move(ends, ue_ref[0 if j == 0 else 1, :, where]).astype(kind)
            for j in range(per):

                @pl.when(s_ref[SENDS + j] == 1)
                def _(j=j, piece=pieces[j]):
                    messages[j][:, where] = piece.astype(BF)

            second = slice((4 + g) * cols, (5 + g) * cols)
            for code, j in ((1, 0), (2, per - 1)):

                @pl.when(s_ref[SENDS + per] == code)
                def _(piece=pieces[j]):
                    both_ref[:, second] = piece.astype(BF)


def seams_kernel(s_ref, *refs, rounds, rows, bands):
    got, refs = refs[:rounds], refs[rounds:]
    first_msg, last_msg, cl_ref, up_ref, down_ref, top_ref, bot_ref, pick_ref, srow_ref, scol_ref = refs[:10]
    rows_ref, unit0_ref, unit7_ref, other_ref, corner_ref = refs[10:]
    faces, (chans, cols) = up_ref.shape[0] - 1, up_ref.shape[1:]
    per = rounds - 1
    span = rows + 2
    first_band = s_ref[BAND] == 0
    kind = F32 if chans % 16 else BF
    lane = lax.broadcasted_iota(jnp.int32, (chans, cols), 1)
    for r in range(rounds):

        @pl.when(s_ref[COL_ROUND] == r)
        def _(r=r):
            other_ref[...] = got[r][:, got[r].shape[1] - 4 * cols :]

    @pl.when((s_ref[COL_ROUND] == rounds) & first_band)
    def _():
        other_ref[...] = first_msg[...]

    @pl.when((s_ref[COL_ROUND] == rounds) & jnp.logical_not(first_band))
    def _():
        other_ref[...] = last_msg[...]

    scol_ref[...] = move(side_by_side(other_ref[...], cl_ref[...]), pick_ref[...]).astype(BF)

    on_row = jnp.logical_or(first_band, s_ref[BAND] == bands - 1)
    table = SENDS + rounds

    @pl.when(on_row)
    def _():
        for code, to, normal in ((FIRST_FROM, unit0_ref, got[0]), (LAST_FROM, unit7_ref, got[per - 1])):
            for value, src in enumerate((normal, got[per], cl_ref)):

                @pl.when(s_ref[code] == value)
                def _(to=to, src=src):
                    to[...] = src[:, : 4 * cols]

        for f in range(faces + 1):
            rows_ref[f] = pick2(first_band, up_ref[f], bot_ref[f])
            rows_ref[faces + 1 + f] = pick2(first_band, top_ref[f], down_ref[f])
        units = [unit0_ref, *got[1 : per - 1], unit7_ref]
        corner_ref[...] = jnp.zeros_like(corner_ref)
        for f in range(faces):
            side, face = s_ref[table + f], s_ref[table + faces + f]

            @pl.when(side < 2)
            def _(f=f, side=side, face=face):
                srow_ref[f] = rows_ref[side * (faces + 1) + face]
                ends = rows_ref[side * (faces + 1) + faces].astype(F32)
                ends = pltpu.roll(ends, lax.rem(2 * f + 2 * cols - 2 * face, cols), 1)
                corner_ref[...] = jnp.where((lane == 2 * f) | (lane == 2 * f + 1), ends, corner_ref[...])

            @pl.when(side >= 2)
            def _(f=f, side=side, face=face):
                group = pl.ds(pl.multiple_of(((side - 2) * 2 + face // 6) * cols, cols), cols)
                q = lax.rem(face, 6) * span
                line = jnp.zeros((chans, cols), kind)
                ends = corner_ref[...]
                for j in range(per):
                    value = units[j][:, group].astype(kind)
                    line = jnp.where(lane // rows == j, pltpu.roll(value, lax.rem(rows * j + 2 * cols - 1 - q, cols), 1), line)
                    if j == 0:
                        ends = jnp.where(lane == 2 * f, pltpu.roll(value.astype(F32), lax.rem(2 * f + 2 * cols - q, cols), 1), ends)
                    if j == per - 1:
                        shift = lax.rem(2 * f + 1 + 2 * cols - q - (span - 1), cols)
                        ends = jnp.where(lane == 2 * f + 1, pltpu.roll(value.astype(F32), shift, 1), ends)
                srow_ref[f] = line.astype(BF)
                corner_ref[...] = ends

        srow_ref[faces] = corner_ref[...].astype(BF)

    @pl.when(jnp.logical_not(on_row))
    def _():
        srow_ref[...] = jnp.zeros_like(srow_ref)


def halo_kernel(s_ref, srow_ref, rrow_ref, scol_ref, rcol_ref, top_ref, bot_ref, left_ref, right_ref, join_ref, joinend_ref, back_ref, widen_ref, ends_ref, t_out, b_out, l_out, r_out, *, bands, tiles, rounds):
    faces, (chans, cols) = top_ref.shape[0] - 1, top_ref.shape[1:]
    first_band, last_band = s_ref[BAND] == 0, s_ref[BAND] == bands - 1
    first_tile, last_tile = s_ref[TILE] == 0, s_ref[TILE] == tiles - 1
    table = SENDS + rounds + 2 * faces
    for cond, out, ref in ((first_band, t_out, top_ref), (last_band, b_out, bot_ref)):

        @pl.when(cond)
        def _(out=out):
            for f in range(faces):
                turned = move(rrow_ref[f], back_ref[...]).astype(BF)
                out[f] = pick2(s_ref[table + f] == 1, turned, srow_ref[f])

        @pl.when(jnp.logical_not(cond))
        def _(out=out, ref=ref):
            for f in range(faces):
                out[f] = ref[f]

    ends = move(side_by_side(srow_ref[faces], rrow_ref[faces]), joinend_ref[...]).astype(BF)
    top_end = pick2(first_band, ends, top_ref[faces])
    bot_end = pick2(last_band, ends, bot_ref[faces])
    none = jnp.zeros_like(top_end)
    seam = move(side_by_side(scol_ref[...], rcol_ref[...]), join_ref[...])
    for side, (at_edge, src, out) in enumerate(((first_tile, left_ref, l_out), (last_tile, right_ref, r_out))):
        use_top = jnp.logical_or(first_band, jnp.logical_not(at_edge))
        use_bot = jnp.logical_or(last_band, jnp.logical_not(at_edge))
        both = side_by_side(pick2(use_top, top_end, none), pick2(use_bot, bot_end, none))
        base = pick2(at_edge, seam, move(src[...], widen_ref[...]))
        out[...] = (base + move(both, ends_ref[side])).astype(BF)


def exchange(x, low, high, plan, tables):
    scalars, pick, join, join_end, (own, wrap, widen, ends, corner, unit_ends, back) = tables
    faces, rows, chans, cols = x.shape
    bands, tiles = plan.bands, plan.tiles
    rounds = len(plan.pairs)
    across = [(i, (i + 1) % tiles) for i in range(tiles)]
    left = lax.ppermute(high, "tile", across)
    right = lax.ppermute(low, "tile", [(j, i) for i, j in across])
    up, down = rows_call(x, left, right, corner)
    around = [(i, (i + 1) % bands) for i in range(bands)]
    top = lax.ppermute(down, "band", around)
    bottom = lax.ppermute(up, "band", [(j, i) for i, j in around])
    outs = whole(
        functools.partial(lines_kernel, bands=bands, rows=rows),
        [(chans, 4 * cols)] * plan.per + [(chans, 8 * cols), (chans, 4 * cols)],
        [],
        scalars, up, down, top, bottom, low, high, left, right, own, wrap, unit_ends,
    )
    messages, col_lines = outs[:-1], outs[-1]
    got = [lax.ppermute(m, AXES, pairs) for m, pairs in zip(messages, plan.pairs)]
    line = (faces + 1, chans, cols)
    srow, scol = whole(
        functools.partial(seams_kernel, rounds=rounds, rows=rows, bands=bands),
        [line, (chans, 2 * cols)],
        [
            pltpu.VMEM((2 * (faces + 1), chans, cols), BF),
            pltpu.VMEM((chans, 4 * cols), BF),
            pltpu.VMEM((chans, 4 * cols), BF),
            pltpu.VMEM((chans, 4 * cols), BF),
            pltpu.VMEM((chans, cols), F32),
        ],
        scalars, *got, messages[0], messages[plan.per - 1], col_lines, up, down, top, bottom, pick,
    )
    rrow = lax.ppermute(srow, AXES, plan.flip_row)
    rcol = lax.ppermute(scol, AXES, plan.flip_col)
    rim = (faces, chans, cols)
    return whole(
        functools.partial(halo_kernel, bands=bands, tiles=tiles, rounds=rounds),
        [rim, rim, (chans, 2 * cols), (chans, 2 * cols)],
        [],
        scalars, srow, rrow, scol, rcol, top, bottom, left, right, join, join_end, back, widen, ends,
    )


def local(
    source,
    regrid_weights,
    dest_group,
    dest_block,
    seam_table,
    conv1_weight,
    conv1_bias,
    conv2_weight,
    conv2_bias,
):
    bands, tiles = lax.axis_size("band"), lax.axis_size("tile")
    devices = bands * tiles
    src_count, top_count, block_len = regrid_weights.shape[:3]
    capacity = 3 * src_count * top_count // devices
    rows = block_len * tiles // bands
    faces = seam_table.shape[0]
    slots_dev = faces * rows
    fields = source.shape[0]
    hid = conv1_weight.shape[1]
    items = src_count * top_count
    total = devices * capacity

    target = dest_group.reshape(items)
    order = jnp.arange(items)
    same = (target[:, None] == target[None, :]) & (order[None, :] < order[:, None])
    position = target * capacity + jnp.sum(same.astype(jnp.int32), axis=1)
    hit = position[:, None] == jnp.arange(total)[None, :]
    out_slots = slots_dev + jnp.sum(
        jnp.where(hit, (dest_block.reshape(items) - slots_dev)[:, None], 0), axis=0
    )
    slots = lax.all_to_all(out_slots.reshape(devices, capacity), AXES, split_axis=0, concat_axis=0, tiled=True)
    outgoing = regrid(source, regrid_weights, position, total)
    arrived = lax.all_to_all(
        outgoing.reshape(devices, capacity, fields, block_len), AXES, split_axis=0, concat_axis=0, tiled=True
    )
    regridded, low, high = place(arrived.reshape(total, fields, block_len), slots.reshape(total), slots_dev)
    regridded = regridded.reshape(faces, rows, fields, block_len)

    plan = Plan(bands, tiles)
    tables = seam_tables(seam_table, plan, rows, block_len)
    depth1 = -(-3 * fields // 128) * 128
    weight1 = wide_weight(conv1_weight, depth1)
    weight2 = wide_weight(conv2_weight, 3 * hid)
    bias1 = jnp.concatenate([conv1_bias, conv1_bias])[:, None]
    bias2 = jnp.concatenate([conv2_bias, conv2_bias])[:, None]
    halo = exchange(regridded, low, high, plan, tables)
    hidden, low, high = conv(regridded, *halo, weight1, bias1, False)
    halo = exchange(hidden, low, high, plan, tables)
    return conv(hidden, *halo, weight2, bias2, True)


def solution(mesh):
    return jax.shard_map(
        local,
        mesh=mesh,
        in_specs=(
            P(None, AXES),
            P(AXES, None, None, None),
            P(AXES, None),
            P(AXES, None),
            P(),
            P(),
            P(),
            P(),
            P(),
        ),
        out_specs=P(None, None, "band", "tile"),
        check_vma=False,
    )
```

```python
import functools

import jax
import jax.numpy as jnp
import numpy as np
from jax import lax
from jax.experimental import pallas as pl
from jax.experimental.pallas import tpu as pltpu
from jax.sharding import PartitionSpec as P

BF = jnp.bfloat16
F32 = jnp.float32
AXES = ("band", "tile")
VMEM_LIMIT = 56 * 1024 * 1024


def regrid_kernel(pos_ref, src_ref, w_ref, out_ref, *, blocks, top, length):
    step = pl.program_id(0)
    for s in range(blocks):
        lhs = src_ref[:, s * length : (s + 1) * length]
        rhs = jnp.concatenate([w_ref[s, k] for k in range(top)], axis=1)
        val = jnp.dot(lhs, rhs, preferred_element_type=F32).astype(BF)
        for k in range(top):
            where = pos_ref[(step * blocks + s) * top + k]
            out_ref[where] = val[:, k * length : (k + 1) * length]


def regrid(source, weights, position, slots):
    fields = source.shape[0]
    count, top, length = weights.shape[0], weights.shape[1], weights.shape[2]
    blocks = 8
    return pl.pallas_call(
        functools.partial(regrid_kernel, blocks=blocks, top=top, length=length),
        grid_spec=pltpu.PrefetchScalarGridSpec(
            num_scalar_prefetch=1,
            grid=(count // blocks,),
            in_specs=[
                pl.BlockSpec((fields, blocks * length), lambda i, p: (0, i)),
                pl.BlockSpec((blocks, top, length, length), lambda i, p: (i, 0, 0, 0)),
            ],
            out_specs=pl.BlockSpec((slots, fields, length), lambda i, p: (0, 0, 0)),
        ),
        out_shape=jax.ShapeDtypeStruct((slots, fields, length), BF),
        compiler_params=pltpu.CompilerParams(vmem_limit_bytes=VMEM_LIMIT),
        cost_estimate=pl.CostEstimate(
            flops=2 * count * top * length * length * fields, bytes_accessed=17_000_000, transcendentals=0
        ),
    )(position, source, weights)


def edge_columns(piece, lane, at, low, high):
    cols = piece.shape[1]
    here = lane == at
    low = jnp.where(here, pltpu.roll(piece, at, 1) if at else piece, low)
    high = jnp.where(here, pltpu.roll(piece, (at + 1) % cols, 1), high)
    return low, high


def place_kernel(slot_ref, in_ref, out_ref, low_ref, high_ref, acc_ref, acc2_ref, *, chunk):
    step = pl.program_id(0)

    @pl.when(step == 0)
    def _():
        acc_ref[...] = jnp.zeros_like(acc_ref)
        acc2_ref[...] = jnp.zeros_like(acc2_ref)

    def body(i, carry):
        for j, ref in ((2 * i, acc_ref), (2 * i + 1, acc2_ref)):
            where = slot_ref[step * chunk + j]
            ref[where] += in_ref[j].astype(F32)
        return carry

    lax.fori_loop(0, chunk // 2, body, 0, unroll=8)

    @pl.when(step == pl.num_programs(0) - 1)
    def _():
        count, chans, cols = out_ref.shape
        lane = lax.broadcasted_iota(jnp.int32, (chans, cols), 1)
        for half in range(2):
            low = high = jnp.zeros((chans, cols), F32)
            for at in range(min(cols, count - half * cols)):
                piece = acc_ref[half * cols + at] + acc2_ref[half * cols + at]
                out_ref[half * cols + at] = piece.astype(BF)
                low, high = edge_columns(piece, lane, at, low, high)
            low_ref[:, half * cols : (half + 1) * cols] = low.astype(BF)
            high_ref[:, half * cols : (half + 1) * cols] = high.astype(BF)


def place(arrived, slots, count):
    items, fields, length = arrived.shape
    chunk = 96
    return pl.pallas_call(
        functools.partial(place_kernel, chunk=chunk),
        grid_spec=pltpu.PrefetchScalarGridSpec(
            num_scalar_prefetch=1,
            grid=(items // chunk,),
            in_specs=[pl.BlockSpec((chunk, fields, length), lambda i, p: (i, 0, 0))],
            out_specs=[
                pl.BlockSpec((count, fields, length), lambda i, p: (0, 0, 0)),
                pl.BlockSpec((fields, 2 * length), lambda i, p: (0, 0)),
                pl.BlockSpec((fields, 2 * length), lambda i, p: (0, 0)),
            ],
            scratch_shapes=[pltpu.VMEM((count + 1, fields, length), F32)] * 2,
        ),
        out_shape=[
            jax.ShapeDtypeStruct((count, fields, length), BF),
            jax.ShapeDtypeStruct((fields, 2 * length), BF),
            jax.ShapeDtypeStruct((fields, 2 * length), BF),
        ],
        compiler_params=pltpu.CompilerParams(vmem_limit_bytes=VMEM_LIMIT),
    )(slots, arrived)


def gelu(v):
    return 0.5 * v * (1.0 + lax.erf(v * np.float32(1.0 / np.sqrt(2.0))))


def conv_kernel(w_ref, b_ref, x_ref, top_ref, bot_ref, l_ref, r_ref, *refs, last):
    if not last:
        edge_ref, refs = refs[0], refs[1:]
    if last:
        o_ref, p_ref, s_ref = refs
    else:
        o_ref, low_ref, high_ref, p_ref = refs
    faces, rows, chans, cols = x_ref.shape
    depth = p_ref.shape[1]
    hid = b_ref.shape[0] // 2
    pitch = hid + 8
    step = pl.program_id(0)
    lane = lax.broadcasted_iota(jnp.int32, (chans, cols), 1)
    spare = depth - 3 * chans
    span = rows + 2
    group = pl.ds(pl.multiple_of((step // 3) * cols, cols), cols)
    back = lax.rem(cols - lax.rem(step, 3) * (faces * span), cols)
    kind = F32 if chans % 16 else BF
    left = pltpu.roll(l_ref[:, group].astype(F32), back, 1).astype(kind)
    right = pltpu.roll(r_ref[:, group].astype(F32), back, 1).astype(kind)
    for f in range(faces):
        for r in range(span):
            row = top_ref[f] if r == 0 else bot_ref[f] if r == rows + 1 else x_ref[f, r - 1]
            mid = row.astype(kind)
            at = f * span + r
            lo = jnp.where(lane == 0, left[:, at : at + 1], pltpu.roll(mid, 1, 1))
            hi = jnp.where(lane == cols - 1, right[:, at : at + 1], pltpu.roll(mid, cols - 1, 1))
            parts = [lo, mid, hi]
            if spare:
                parts.append(jnp.zeros((spare, cols), F32))
            p_ref[r, :, f * cols : (f + 1) * cols] = jnp.concatenate(parts, axis=0).astype(BF)
    bias = b_ref[...]
    edges = jnp.zeros((2 * hid, 2 * cols), F32)
    for rp in range(rows // 2):
        patch = p_ref[2 * rp : 2 * rp + 4].reshape(4 * depth, faces * cols)
        acc = jnp.dot(w_ref[...], patch, preferred_element_type=F32) + bias
        acc = gelu(acc)
        if not last:
            acc = acc.astype(BF)
            edges += jnp.dot(acc, edge_ref[rp], preferred_element_type=F32)
        for d in range(2):
            for f in range(faces):
                piece = acc[d * hid : (d + 1) * hid, f * cols : (f + 1) * cols]
                if last:
                    s_ref[f, (2 * rp + d) * pitch : (2 * rp + d) * pitch + hid, :] = piece
                else:
                    o_ref[f, 2 * rp + d] = piece
    if last:
        for f in range(faces):
            for o in range(hid):
                o_ref[o, f] = s_ref[f, pl.ds(o, rows, stride=pitch), :].astype(BF)
    else:
        per = cols // (faces * rows)
        ahead = lax.rem(step, per) * (faces * rows)
        half = pl.ds(pl.multiple_of((step // per) * cols, cols), cols)
        fresh = lax.rem(step, per) == 0
        for i, ref in enumerate((low_ref, high_ref)):
            value = edges[:hid, i * cols : (i + 1) * cols] + pltpu.roll(edges[hid:, i * cols : (i + 1) * cols], 1, 1)
            value = pltpu.roll(value, ahead, 1).astype(BF)

            @pl.when(fresh)
            def _(ref=ref, value=value):
                ref[:, half] = value

            @pl.when(jnp.logical_not(fresh))
            def _(ref=ref, value=value):
                ref[:, half] += value


def edge_maps(faces, rows, cols):
    maps = np.zeros((rows // 2, faces * cols, 2 * cols), np.float32)
    for rp in range(rows // 2):
        for f in range(faces):
            maps[rp, f * cols, f * rows + 2 * rp] = 1
            maps[rp, f * cols + cols - 1, cols + f * rows + 2 * rp] = 1
    return jnp.asarray(maps, BF)


def conv(x, top, bottom, left, right, weight, bias, last):
    face_count, rows, chans, cols = x.shape
    depth = weight.shape[1] // 4
    hid = weight.shape[0] // 2
    faces = 2
    scratch = [pltpu.VMEM((rows + 2, depth, faces * cols), BF)]
    if last:
        out_shape = jax.ShapeDtypeStruct((hid, face_count, rows, cols), BF)
        out_spec = pl.BlockSpec((hid, faces, rows, cols), lambda i: (0, i, 0, 0))
        scratch.append(pltpu.VMEM((faces, rows * (hid + 8), cols), F32))
    else:
        out_shape = [jax.ShapeDtypeStruct((face_count, rows, hid, cols), BF)]
        out_shape += [jax.ShapeDtypeStruct((hid, 2 * cols), BF)] * 2
        out_spec = [pl.BlockSpec((faces, rows, hid, cols), lambda i: (i, 0, 0, 0))]
        out_spec += [pl.BlockSpec((hid, 2 * cols), lambda i: (0, 0))] * 2
    return pl.pallas_call(
        functools.partial(conv_kernel, last=last),
        grid=(face_count // faces,),
        in_specs=[
            pl.BlockSpec(weight.shape, lambda i: (0, 0)),
            pl.BlockSpec(bias.shape, lambda i: (0, 0)),
            pl.BlockSpec((faces, rows, chans, cols), lambda i: (i, 0, 0, 0)),
            pl.BlockSpec((faces, chans, cols), lambda i: (i, 0, 0)),
            pl.BlockSpec((faces, chans, cols), lambda i: (i, 0, 0)),
            pl.BlockSpec(left.shape, lambda i: (0, 0)),
            pl.BlockSpec(right.shape, lambda i: (0, 0)),
        ]
        + ([] if last else [pl.BlockSpec((rows // 2, faces * cols, 2 * cols), lambda i: (0, 0, 0))]),
        out_specs=out_spec,
        out_shape=out_shape,
        scratch_shapes=scratch,
        compiler_params=pltpu.CompilerParams(vmem_limit_bytes=VMEM_LIMIT),
    )(weight, bias, x, top, bottom, left, right, *([] if last else [edge_maps(faces, rows, cols)]))


def wide_weight(weight, depth):
    taps, hid, chans = weight.shape
    rows = weight.reshape(3, 3, hid, chans).transpose(2, 0, 1, 3).reshape(hid, 3, 3 * chans)
    rows = jnp.pad(rows, ((0, 0), (0, 0), (0, depth - 3 * chans)))
    first = jnp.pad(rows, ((0, 0), (0, 1), (0, 0)))
    second = jnp.pad(rows, ((0, 0), (1, 0), (0, 0)))
    return jnp.stack([first, second]).reshape(2 * hid, 4 * depth)


class Plan:
    def __init__(self, bands, tiles):
        self.bands, self.tiles = bands, tiles
        self.per = bands // tiles
        per, last = self.per, bands - 1
        rounds = per + 1
        count = bands * tiles
        self.pairs = [[] for _ in range(rounds)]
        self.sends = np.zeros((rounds, count), np.int32)
        self.row_from = np.full((count, per), 2, np.int32)
        self.col_round = np.full((count,), rounds, np.int32)
        near, far = 0, last * tiles + tiles - 1
        corners = (tiles - 1, last * tiles)
        self.pairs[0].append((near, corners[1]))
        self.pairs[per - 1].append((far, corners[0]))
        self.pairs[per] = [(near, corners[0]), (far, corners[1])]
        self.sends[per, near], self.sends[per, far] = 1, 2

        def join(row_dev, col_dev, j):
            if row_dev in corners and col_dev in corners:
                self.row_from[row_dev, j] = 0
                self.col_round[col_dev] = per
            elif row_dev != col_dev:
                self.sends[j, row_dev] = 1
                self.pairs[j] += [(row_dev, col_dev), (col_dev, row_dev)]
                self.row_from[row_dev, j] = 0
                self.col_round[col_dev] = j

        for j in range(per):
            for t in range(tiles):
                join(t, (per * t + j) * tiles, j)
                join(last * tiles + t, (per * t + j) * tiles + tiles - 1, j)
        for pairs in self.pairs:
            assert len({a for a, _ in pairs}) == len(pairs) == len({b for _, b in pairs})
        self.flip_row = [
            (b * tiles + t, b * tiles + tiles - 1 - t) for b in (0, last) for t in range(tiles)
        ]
        self.flip_col = [(b * tiles + t, (last - b) * tiles + t) for b in range(bands) for t in (0, tiles - 1)]


def lane18(f, p, span, width):
    return (f // 6) * width + (f % 6) * span + p


def fixed_maps(faces, rows, cols):
    span = rows + 2
    own = np.zeros((3 * cols, 2 * cols), np.float32)
    wrap = np.zeros((4 * cols, 2 * cols), np.float32)
    widen = np.zeros((2 * cols, 2 * cols), np.float32)
    ends = np.zeros((2, 2 * cols, 2 * cols), np.float32)
    corner = np.zeros((2, 4 * cols, cols), np.float32)
    unit_ends = np.zeros((2, 2 * cols, 4 * cols), np.float32)
    for f in range(faces):
        for r in range(rows):
            to = lane18(f, r + 1, span, cols)
            own[f * rows + r, to] = wrap[f * rows + r, to] = widen[f * rows + r, to] = 1
        for which, p in ((0, 0), (1, span - 1)):
            to = lane18(f, p, span, cols)
            own[2 * cols + 16 * which + f, to] = 1
            wrap[(2 + which) * cols + 2 * f, to] = 1
            for side in range(2):
                ends[side, which * cols + 2 * f + side, to] = 1
        for which, r in ((0, 0), (1, rows - 1)):
            for side in range(2):
                corner[which, side * 2 * cols + f * rows + r, 2 * f + side] = 1
        for which, p in ((0, 0), (1, span - 1)):
            for pair in range(2):
                to = pair * 2 * cols + lane18(f, p, span, cols)
                unit_ends[which, pair * cols + 2 * f + which, to] = 1
    back = np.eye(cols)[::-1].copy()
    return [jnp.asarray(m, BF) for m in (own, wrap, widen, ends, corner, unit_ends, back)]


def seam_tables(seam_table, plan, rows, cols):
    band, tile = lax.axis_index("band"), lax.axis_index("tile")
    me = band * plan.tiles + tile
    faces = seam_table.shape[0]
    span = rows + 2
    per, rounds = plan.per, plan.per + 1
    last_band, last_tile = plan.bands - 1, plan.tiles - 1
    static = np.concatenate(
        [
            plan.col_round[:, None],
            plan.row_from[:, :1],
            plan.row_from[:, -1:],
            plan.sends.T,
        ],
        axis=1,
    ).astype(np.int32)
    static = lax.dynamic_slice_in_dim(jnp.asarray(static), me, 1, 0)[0]
    row = jnp.where(band == 0, seam_table[:, 0], seam_table[:, 1])
    col = jnp.where(tile == 0, seam_table[:, 2], seam_table[:, 3])
    scalars = jnp.concatenate(
        [jnp.stack([band, tile]).astype(jnp.int32), static, row[:, 1], row[:, 0], row[:, 2], jnp.zeros((4,), jnp.int32)]
    )
    lanes = np.full((2, 2 * cols), -1, np.int32)
    for f in range(faces):
        for p in range(span):
            lanes[:, lane18(f, p, span, cols)] = f, p
    face, place = lanes
    line_in = np.concatenate([np.where(face >= 0, face + faces * side, -1) for side in range(4)])
    place_in = np.tile(place, 4)
    col_line = col[:, 1] * faces + col[:, 0]
    hot = jnp.asarray(face[:, None] == np.arange(faces)[None, :])
    want = jnp.sum(jnp.where(hot, col_line[None, :], 0), axis=1)
    turned = jnp.sum(jnp.where(hot, col[:, 2][None, :], 0), axis=1)
    pick = (jnp.asarray(line_in)[:, None] == want[None, :]) & jnp.asarray(
        (place_in[:, None] == place[None, :]) & (face >= 0)[None, :]
    )
    corner = ((band == 0) & jnp.asarray(place == 0)) | ((band == last_band) & jnp.asarray(place == span - 1))
    same_face = (face[:, None] == face[None, :]) & (face >= 0)[None, :]
    keep = jnp.asarray(same_face & (place[:, None] == place[None, :])) & (turned == 0)[None, :]
    flip = jnp.asarray(same_face & (place[:, None] == span - 1 - place[None, :])) & (turned == 1)[None, :]
    join = jnp.concatenate([keep, flip]) & jnp.logical_not(corner)[None, :]
    at = np.arange(cols)
    end_face, end_side = np.where(at < 2 * faces, at // 2, -1), at % 2
    end_turned = jnp.sum(jnp.where(jnp.asarray(end_face[:, None] == np.arange(faces)[None, :]), row[:, 2][None, :], 0), axis=1)
    outer = ((tile == 0) & jnp.asarray(end_side == 0)) | ((tile == last_tile) & jnp.asarray(end_side == 1))
    same_end = (end_face[:, None] == end_face[None, :]) & (end_face >= 0)[None, :]
    keep_end = jnp.asarray(same_end & (end_side[:, None] == end_side[None, :])) & (end_turned == 0)[None, :]
    flip_end = jnp.asarray(same_end & (end_side[:, None] != end_side[None, :])) & (end_turned == 1)[None, :]
    join_end = jnp.concatenate([keep_end, flip_end]) & jnp.logical_not(outer)[None, :]
    return scalars, pick.astype(BF), join.astype(BF), join_end.astype(BF), fixed_maps(faces, rows, cols)


BAND, TILE, COL_ROUND, FIRST_FROM, LAST_FROM, SENDS = 0, 1, 2, 3, 4, 5


def whole(kernel, out_shape, scratch, scalars, *args):
    return pl.pallas_call(
        kernel,
        in_specs=[pl.BlockSpec(memory_space=pltpu.SMEM)] + [pl.BlockSpec(memory_space=pltpu.VMEM)] * len(args),
        out_specs=[pl.BlockSpec(memory_space=pltpu.VMEM)] * len(out_shape),
        out_shape=[jax.ShapeDtypeStruct(s, BF) for s in out_shape],
        scratch_shapes=scratch,
        compiler_params=pltpu.CompilerParams(vmem_limit_bytes=VMEM_LIMIT),
    )(scalars, *args)


def pick2(cond, a, b):
    return lax.select_n(cond, b, a)


def side_by_side(*parts):
    return jnp.concatenate(parts, axis=1)


def move(x, matrix):
    return jnp.dot(x, matrix, preferred_element_type=F32)


def rows_kernel(first_ref, last_ref, left_ref, right_ref, corner_ref, up_ref, down_ref):
    faces = first_ref.shape[0]
    both = side_by_side(left_ref[...], right_ref[...])
    for which, (src, out) in enumerate(((first_ref, up_ref), (last_ref, down_ref))):
        for f in range(faces):
            out[f] = src[f, 0]
        out[faces] = move(both, corner_ref[which]).astype(BF)


def rows_call(x, left, right, corner):
    faces, rows, chans, cols = x.shape
    full = lambda a: pl.BlockSpec(a.shape, lambda i: (0,) * a.ndim)
    out = jax.ShapeDtypeStruct((faces + 1, chans, cols), BF)
    return pl.pallas_call(
        rows_kernel,
        grid=(1,),
        in_specs=[
            pl.BlockSpec((faces, 1, chans, cols), lambda i: (0, 0, 0, 0)),
            pl.BlockSpec((faces, 1, chans, cols), lambda i: (0, rows - 1, 0, 0)),
            full(left),
            full(right),
            full(corner),
        ],
        out_specs=[pl.BlockSpec(out.shape, lambda i: (0, 0, 0))] * 2,
        out_shape=[out] * 2,
        compiler_params=pltpu.CompilerParams(vmem_limit_bytes=VMEM_LIMIT),
    )(x, x, left, right, corner)


def lines_kernel(s_ref, up_ref, down_ref, top_ref, bot_ref, low_ref, high_ref, left_ref, right_ref, own_ref, wrap_ref, ue_ref, *outs, bands, rows):
    messages, extra_ref, cl_ref = outs[:-2], outs[-2], outs[-1]
    per = len(messages)
    faces, (chans, cols) = up_ref.shape[0] - 1, up_ref.shape[1:]
    span = rows + 2
    kind = F32 if chans % 16 else BF
    first_band, first_tile = s_ref[BAND] == 0, s_ref[TILE] == 0
    lane = lax.broadcasted_iota(jnp.int32, (chans, cols), 1)
    top_edge = jnp.zeros((chans, cols), F32)
    for which, ref in enumerate((top_ref, bot_ref)):
        for f in range(faces):
            at = 16 * which + f
            row = ref[f].astype(F32)
            value = pltpu.roll(row, pick2(first_tile, jnp.int32(at), jnp.int32(at + 1)), 1)
            top_edge = jnp.where(lane == at, value, top_edge)
    mine = pick2(first_tile, low_ref[...], high_ref[...])
    theirs = pick2(first_tile, left_ref[...], right_ref[...])
    turn = pick2(first_tile, jnp.int32(0), jnp.int32(cols - 1))
    tc = pltpu.roll(top_ref[faces].astype(F32), turn, 1).astype(BF)
    bc = pltpu.roll(bot_ref[faces].astype(F32), turn, 1).astype(BF)
    own = move(side_by_side(mine, top_edge.astype(BF)), own_ref[...]).astype(BF)
    wrap = move(side_by_side(theirs, tc, bc), wrap_ref[...]).astype(BF)
    cl_ref[...] = side_by_side(pick2(first_tile, own, wrap), pick2(first_tile, wrap, own))
    on_row = jnp.logical_or(first_band, s_ref[BAND] == bands - 1)
    extra_ref[...] = jnp.zeros_like(extra_ref)
    for m in range(per):

        @pl.when(s_ref[SENDS + m] == 0)
        def _(m=m):
            messages[m][...] = cl_ref[...]

    @pl.when(on_row)
    def _():
        ends = side_by_side(pick2(first_band, up_ref[faces], bot_ref[faces]), pick2(first_band, top_ref[faces], down_ref[faces]))
        for g in range(4):
            pieces = [jnp.zeros((chans, cols), kind) for _ in range(per)]
            for i in range(6):
                pair, f = divmod(6 * g + i, faces)
                line = pick2(first_band, up_ref[f], bot_ref[f]) if pair == 0 else pick2(first_band, top_ref[f], down_ref[f])
                line = line.astype(kind)
                for j in range(per):
                    low = i * span + (1 if j == 0 else 0)
                    high = i * span + span - (1 if j == per - 1 else 0)
                    value = pltpu.roll(line, (i * span + 1 - rows * j) % cols, 1)
                    pieces[j] = jnp.where((lane >= low) & (lane < high), value, pieces[j])
            where = slice(g * cols, (g + 1) * cols)
            for j in (0, per - 1):
                pieces[j] = pieces[j] + move(ends, ue_ref[0 if j == 0 else 1, :, where]).astype(kind)
            for j in range(per):

                @pl.when(s_ref[SENDS + j] == 1)
                def _(j=j, piece=pieces[j]):
                    messages[j][:, where] = piece.astype(BF)

            for code, j in ((1, 0), (2, per - 1)):

                @pl.when(s_ref[SENDS + per] == code)
                def _(piece=pieces[j]):
                    extra_ref[:, where] = piece.astype(BF)


def seams_kernel(s_ref, *refs, rounds, rows, bands):
    got, refs = refs[:rounds], refs[rounds:]
    extra_ref, cl_ref, up_ref, down_ref, top_ref, bot_ref, pick_ref, srow_ref, scol_ref = refs[:9]
    rows_ref, unit0_ref, unit7_ref, other_ref, corner_ref = refs[9:]
    faces, (chans, cols) = up_ref.shape[0] - 1, up_ref.shape[1:]
    per = rounds - 1
    span = rows + 2
    first_band = s_ref[BAND] == 0
    kind = F32 if chans % 16 else BF
    lane = lax.broadcasted_iota(jnp.int32, (chans, cols), 1)
    for r in range(rounds):

        @pl.when(s_ref[COL_ROUND] == r)
        def _(r=r):
            other_ref[...] = got[r][...]

    @pl.when(s_ref[COL_ROUND] == rounds)
    def _():
        other_ref[...] = extra_ref[...]

    scol_ref[...] = move(side_by_side(other_ref[...], cl_ref[...]), pick_ref[...]).astype(BF)

    on_row = jnp.logical_or(first_band, s_ref[BAND] == bands - 1)
    table = SENDS + rounds

    @pl.when(on_row)
    def _():
        for code, to, normal in ((FIRST_FROM, unit0_ref, got[0]), (LAST_FROM, unit7_ref, got[per - 1])):
            for value, src in ((0, normal), (2, cl_ref)):

                @pl.when(s_ref[code] == value)
                def _(to=to, src=src):
                    to[...] = src[...]

        for f in range(faces + 1):
            rows_ref[f] = pick2(first_band, up_ref[f], bot_ref[f])
            rows_ref[faces + 1 + f] = pick2(first_band, top_ref[f], down_ref[f])
        units = [unit0_ref, *got[1 : per - 1], unit7_ref]
        corner_ref[...] = jnp.zeros_like(corner_ref)
        for f in range(faces):
            side, face = s_ref[table + f], s_ref[table + faces + f]

            @pl.when(side < 2)
            def _(f=f, side=side, face=face):
                srow_ref[f] = rows_ref[side * (faces + 1) + face]
                ends = rows_ref[side * (faces + 1) + faces].astype(F32)
                ends = pltpu.roll(ends, lax.rem(2 * f + 2 * cols - 2 * face, cols), 1)
                corner_ref[...] = jnp.where((lane == 2 * f) | (lane == 2 * f + 1), ends, corner_ref[...])

            @pl.when(side >= 2)
            def _(f=f, side=side, face=face):
                group = pl.ds(pl.multiple_of(((side - 2) * 2 + face // 6) * cols, cols), cols)
                q = lax.rem(face, 6) * span
                line = jnp.zeros((chans, cols), kind)
                ends = corner_ref[...]
                for j in range(per):
                    value = units[j][:, group].astype(kind)
                    line = jnp.where(lane // rows == j, pltpu.roll(value, lax.rem(rows * j + 2 * cols - 1 - q, cols), 1), line)
                    if j == 0:
                        ends = jnp.where(lane == 2 * f, pltpu.roll(value.astype(F32), lax.rem(2 * f + 2 * cols - q, cols), 1), ends)
                    if j == per - 1:
                        shift = lax.rem(2 * f + 1 + 2 * cols - q - (span - 1), cols)
                        ends = jnp.where(lane == 2 * f + 1, pltpu.roll(value.astype(F32), shift, 1), ends)
                srow_ref[f] = line.astype(BF)
                corner_ref[...] = ends

        srow_ref[faces] = corner_ref[...].astype(BF)

    @pl.when(jnp.logical_not(on_row))
    def _():
        srow_ref[...] = jnp.zeros_like(srow_ref)


def halo_kernel(s_ref, srow_ref, rrow_ref, scol_ref, rcol_ref, top_ref, bot_ref, left_ref, right_ref, join_ref, joinend_ref, back_ref, widen_ref, ends_ref, t_out, b_out, l_out, r_out, *, bands, tiles, rounds):
    faces, (chans, cols) = top_ref.shape[0] - 1, top_ref.shape[1:]
    first_band, last_band = s_ref[BAND] == 0, s_ref[BAND] == bands - 1
    first_tile, last_tile = s_ref[TILE] == 0, s_ref[TILE] == tiles - 1
    table = SENDS + rounds + 2 * faces
    for cond, out, ref in ((first_band, t_out, top_ref), (last_band, b_out, bot_ref)):

        @pl.when(cond)
        def _(out=out):
            for f in range(faces):
                turned = move(rrow_ref[f], back_ref[...]).astype(BF)
                out[f] = pick2(s_ref[table + f] == 1, turned, srow_ref[f])

        @pl.when(jnp.logical_not(cond))
        def _(out=out, ref=ref):
            for f in range(faces):
                out[f] = ref[f]

    ends = move(side_by_side(srow_ref[faces], rrow_ref[faces]), joinend_ref[...]).astype(BF)
    top_end = pick2(first_band, ends, top_ref[faces])
    bot_end = pick2(last_band, ends, bot_ref[faces])
    none = jnp.zeros_like(top_end)
    seam = move(side_by_side(scol_ref[...], rcol_ref[...]), join_ref[...])
    for side, (at_edge, src, out) in enumerate(((first_tile, left_ref, l_out), (last_tile, right_ref, r_out))):
        use_top = jnp.logical_or(first_band, jnp.logical_not(at_edge))
        use_bot = jnp.logical_or(last_band, jnp.logical_not(at_edge))
        both = side_by_side(pick2(use_top, top_end, none), pick2(use_bot, bot_end, none))
        base = pick2(at_edge, seam, move(src[...], widen_ref[...]))
        out[...] = (base + move(both, ends_ref[side])).astype(BF)


def exchange(x, low, high, plan, tables):
    scalars, pick, join, join_end, (own, wrap, widen, ends, corner, unit_ends, back) = tables
    faces, rows, chans, cols = x.shape
    bands, tiles = plan.bands, plan.tiles
    rounds = len(plan.pairs)
    across = [(i, (i + 1) % tiles) for i in range(tiles)]
    left = lax.ppermute(high, "tile", across)
    right = lax.ppermute(low, "tile", [(j, i) for i, j in across])
    up, down = rows_call(x, left, right, corner)
    around = [(i, (i + 1) % bands) for i in range(bands)]
    top = lax.ppermute(down, "band", around)
    bottom = lax.ppermute(up, "band", [(j, i) for i, j in around])
    outs = whole(
        functools.partial(lines_kernel, bands=bands, rows=rows),
        [(chans, 4 * cols)] * plan.per + [(chans, 4 * cols)] * 2,
        [],
        scalars, up, down, top, bottom, low, high, left, right, own, wrap, unit_ends,
    )
    messages, col_lines = outs[:-1], outs[-1]
    got = [lax.ppermute(m, AXES, pairs) for m, pairs in zip(messages, plan.pairs)]
    line = (faces + 1, chans, cols)
    srow, scol = whole(
        functools.partial(seams_kernel, rounds=rounds, rows=rows, bands=bands),
        [line, (chans, 2 * cols)],
        [
            pltpu.VMEM((2 * (faces + 1), chans, cols), BF),
            pltpu.VMEM((chans, 4 * cols), BF),
            pltpu.VMEM((chans, 4 * cols), BF),
            pltpu.VMEM((chans, 4 * cols), BF),
            pltpu.VMEM((chans, cols), F32),
        ],
        scalars, *got, messages[-1], col_lines, up, down, top, bottom, pick,
    )
    rrow = lax.ppermute(srow, AXES, plan.flip_row)
    rcol = lax.ppermute(scol, AXES, plan.flip_col)
    rim = (faces, chans, cols)
    return whole(
        functools.partial(halo_kernel, bands=bands, tiles=tiles, rounds=rounds),
        [rim, rim, (chans, 2 * cols), (chans, 2 * cols)],
        [],
        scalars, srow, rrow, scol, rcol, top, bottom, left, right, join, join_end, back, widen, ends,
    )


def local(
    source,
    regrid_weights,
    dest_group,
    dest_block,
    seam_table,
    conv1_weight,
    conv1_bias,
    conv2_weight,
    conv2_bias,
):
    bands, tiles = lax.axis_size("band"), lax.axis_size("tile")
    devices = bands * tiles
    src_count, top_count, block_len = regrid_weights.shape[:3]
    capacity = 3 * src_count * top_count // devices
    rows = block_len * tiles // bands
    faces = seam_table.shape[0]
    slots_dev = faces * rows
    fields = source.shape[0]
    hid = conv1_weight.shape[1]
    items = src_count * top_count
    total = devices * capacity

    target = dest_group.reshape(items)
    order = jnp.arange(items)
    same = (target[:, None] == target[None, :]) & (order[None, :] < order[:, None])
    position = target * capacity + jnp.sum(same.astype(jnp.int32), axis=1)
    hit = position[:, None] == jnp.arange(total)[None, :]
    out_slots = slots_dev + jnp.sum(
        jnp.where(hit, (dest_block.reshape(items) - slots_dev)[:, None], 0), axis=0
    )
    slots = lax.all_to_all(out_slots.reshape(devices, capacity), AXES, split_axis=0, concat_axis=0, tiled=True)
    outgoing = regrid(source, regrid_weights, position, total)
    arrived = lax.all_to_all(
        outgoing.reshape(devices, capacity, fields, block_len), AXES, split_axis=0, concat_axis=0, tiled=True
    )
    regridded, low, high = place(arrived.reshape(total, fields, block_len), slots.reshape(total), slots_dev)
    regridded = regridded.reshape(faces, rows, fields, block_len)

    plan = Plan(bands, tiles)
    tables = seam_tables(seam_table, plan, rows, block_len)
    depth1 = -(-3 * fields // 128) * 128
    weight1 = wide_weight(conv1_weight, depth1)
    weight2 = wide_weight(conv2_weight, 3 * hid)
    bias1 = jnp.concatenate([conv1_bias, conv1_bias])[:, None]
    bias2 = jnp.concatenate([conv2_bias, conv2_bias])[:, None]
    halo = exchange(regridded, low, high, plan, tables)
    hidden, low, high = conv(regridded, *halo, weight1, bias1, False)
    halo = exchange(hidden, low, high, plan, tables)
    return conv(hidden, *halo, weight2, bias2, True)


def solution(mesh):
    return jax.shard_map(
        local,
        mesh=mesh,
        in_specs=(
            P(None, AXES),
            P(AXES, None, None, None),
            P(AXES, None),
            P(AXES, None),
            P(),
            P(),
            P(),
            P(),
            P(),
        ),
        out_specs=P(None, None, "band", "tile"),
        check_vma=False,
    )
```

```python
import functools

import jax
import jax.numpy as jnp
import numpy as np
from jax import lax
from jax.experimental import pallas as pl
from jax.experimental.pallas import tpu as pltpu
from jax.sharding import PartitionSpec as P

BF = jnp.bfloat16
F32 = jnp.float32
AXES = ("band", "tile")
VMEM_LIMIT = 56 * 1024 * 1024


def regrid_kernel(pos_ref, src_ref, w_ref, slot_ref, out_ref, *, blocks, top, length):
    step = pl.program_id(0)
    fields = src_ref.shape[0]
    count = pl.num_programs(0) * blocks * top

    @pl.when(step == 0)
    def _():
        out_ref[:, out_ref.shape[1] - 1] = slot_ref[...]

    for s in range(blocks):
        lhs = src_ref[:, s * length : (s + 1) * length]
        rhs = jnp.concatenate([w_ref[s, k] for k in range(top)], axis=1)
        val = jnp.dot(lhs, rhs, preferred_element_type=F32)
        for k in range(top):
            item = (step * blocks + s) * top + k
            piece = val[:, k * length : (k + 1) * length].reshape(fields // 8, 8, length)
            out_ref[pos_ref[item], pl.ds(pos_ref[count + item], fields // 8)] = piece.astype(BF)


def regrid(source, weights, position, slots, capacity):
    fields = source.shape[0]
    count, top, length = weights.shape[0], weights.shape[1], weights.shape[2]
    blocks = 8
    shape = (slots.shape[0], capacity * fields // 8 + 1, 8, length)
    return pl.pallas_call(
        functools.partial(regrid_kernel, blocks=blocks, top=top, length=length),
        grid_spec=pltpu.PrefetchScalarGridSpec(
            num_scalar_prefetch=1,
            grid=(count // blocks,),
            in_specs=[
                pl.BlockSpec((fields, blocks * length), lambda i, p: (0, i)),
                pl.BlockSpec((blocks, top, length, length), lambda i, p: (i, 0, 0, 0)),
                pl.BlockSpec(slots.shape, lambda i, p: (0, 0, 0)),
            ],
            out_specs=pl.BlockSpec(shape, lambda i, p: (0, 0, 0, 0)),
        ),
        out_shape=jax.ShapeDtypeStruct(shape, BF),
        compiler_params=pltpu.CompilerParams(vmem_limit_bytes=VMEM_LIMIT),
        cost_estimate=pl.CostEstimate(
            flops=2 * count * top * length * length * fields, bytes_accessed=17_000_000, transcendentals=0
        ),
    )(position, source, weights, slots)


def edge_columns(piece, lane, at, low, high):
    cols = piece.shape[1]
    here = lane == at
    low = jnp.where(here, pltpu.roll(piece, at, 1) if at else piece, low)
    high = jnp.where(here, pltpu.roll(piece, (at + 1) % cols, 1), high)
    return low, high


def place_kernel(slot_ref, in_ref, out_ref, low_ref, high_ref, acc_ref, acc2_ref, *, chunk):
    step = pl.program_id(0)
    tiles = acc_ref.shape[1]
    capacity = in_ref.shape[1] // tiles

    @pl.when(step == 0)
    def _():
        acc_ref[...] = jnp.zeros_like(acc_ref)
        acc2_ref[...] = jnp.zeros_like(acc2_ref)

    def body(i, carry):
        for r in range(capacity):
            ref = acc_ref if r % 2 == 0 else acc2_ref
            where = slot_ref[(step * chunk + i) * capacity + r]
            ref[where] += in_ref[i, r * tiles : (r + 1) * tiles].astype(F32)
        return carry

    lax.fori_loop(0, chunk, body, 0, unroll=2)

    @pl.when(step == pl.num_programs(0) - 1)
    def _():
        count, chans, cols = out_ref.shape
        lane = lax.broadcasted_iota(jnp.int32, (chans, cols), 1)
        for half in range(2):
            low = high = jnp.zeros((chans, cols), F32)
            for at in range(min(cols, count - half * cols)):
                piece = (acc_ref[half * cols + at] + acc2_ref[half * cols + at]).reshape(chans, cols)
                out_ref[half * cols + at] = piece.astype(BF)
                low, high = edge_columns(piece, lane, at, low, high)
            low_ref[:, half * cols : (half + 1) * cols] = low.astype(BF)
            high_ref[:, half * cols : (half + 1) * cols] = high.astype(BF)


def place(arrived, slots, count):
    senders, size, eight, length = arrived.shape
    chunk = 16
    fields = size // (slots.shape[0] // senders) * eight
    return pl.pallas_call(
        functools.partial(place_kernel, chunk=chunk),
        grid_spec=pltpu.PrefetchScalarGridSpec(
            num_scalar_prefetch=1,
            grid=(senders // chunk,),
            in_specs=[pl.BlockSpec((chunk, size, eight, length), lambda i, p: (i, 0, 0, 0))],
            out_specs=[
                pl.BlockSpec((count, fields, length), lambda i, p: (0, 0, 0)),
                pl.BlockSpec((fields, 2 * length), lambda i, p: (0, 0)),
                pl.BlockSpec((fields, 2 * length), lambda i, p: (0, 0)),
            ],
            scratch_shapes=[pltpu.VMEM((count + 1, fields // 8, 8, length), F32)] * 2,
        ),
        out_shape=[
            jax.ShapeDtypeStruct((count, fields, length), BF),
            jax.ShapeDtypeStruct((fields, 2 * length), BF),
            jax.ShapeDtypeStruct((fields, 2 * length), BF),
        ],
        compiler_params=pltpu.CompilerParams(vmem_limit_bytes=VMEM_LIMIT),
    )(slots, arrived)


def gelu(v):
    return 0.5 * v * (1.0 + lax.erf(v * np.float32(1.0 / np.sqrt(2.0))))


def conv_kernel(w_ref, b_ref, x_ref, top_ref, bot_ref, l_ref, r_ref, *refs, last):
    if not last:
        edge_ref, refs = refs[0], refs[1:]
    if last:
        o_ref, p_ref, s_ref = refs
    else:
        o_ref, low_ref, high_ref, p_ref = refs
    faces, rows, chans, cols = x_ref.shape
    depth = p_ref.shape[1]
    hid = b_ref.shape[0] // 2
    pitch = hid + 8
    step = pl.program_id(0)
    lane = lax.broadcasted_iota(jnp.int32, (chans, cols), 1)
    spare = depth - 3 * chans
    span = rows + 2
    group = pl.ds(pl.multiple_of((step // 3) * cols, cols), cols)
    back = lax.rem(cols - lax.rem(step, 3) * (faces * span), cols)
    kind = F32 if chans % 16 else BF
    left = pltpu.roll(l_ref[:, group].astype(F32), back, 1).astype(kind)
    right = pltpu.roll(r_ref[:, group].astype(F32), back, 1).astype(kind)
    for f in range(faces):
        for r in range(span):
            row = top_ref[f] if r == 0 else bot_ref[f] if r == rows + 1 else x_ref[f, r - 1]
            mid = row.astype(kind)
            at = f * span + r
            lo = jnp.where(lane == 0, left[:, at : at + 1], pltpu.roll(mid, 1, 1))
            hi = jnp.where(lane == cols - 1, right[:, at : at + 1], pltpu.roll(mid, cols - 1, 1))
            parts = [lo, mid, hi]
            if spare:
                parts.append(jnp.zeros((spare, cols), F32))
            p_ref[r, :, f * cols : (f + 1) * cols] = jnp.concatenate(parts, axis=0).astype(BF)
    bias = b_ref[...]
    edges = jnp.zeros((2 * hid, 2 * cols), F32)
    for rp in range(rows // 2):
        patch = p_ref[2 * rp : 2 * rp + 4].reshape(4 * depth, faces * cols)
        acc = jnp.dot(w_ref[...], patch, preferred_element_type=F32) + bias
        acc = gelu(acc)
        if not last:
            acc = acc.astype(BF)
            edges += jnp.dot(acc, edge_ref[rp], preferred_element_type=F32)
        for d in range(2):
            for f in range(faces):
                piece = acc[d * hid : (d + 1) * hid, f * cols : (f + 1) * cols]
                if last:
                    s_ref[f, (2 * rp + d) * pitch : (2 * rp + d) * pitch + hid, :] = piece
                else:
                    o_ref[f, 2 * rp + d] = piece
    if last:
        for f in range(faces):
            for o in range(hid):
                o_ref[o, f] = s_ref[f, pl.ds(o, rows, stride=pitch), :].astype(BF)
    else:
        per = cols // (faces * rows)
        ahead = lax.rem(step, per) * (faces * rows)
        half = pl.ds(pl.multiple_of((step // per) * cols, cols), cols)
        fresh = lax.rem(step, per) == 0
        for i, ref in enumerate((low_ref, high_ref)):
            value = edges[:hid, i * cols : (i + 1) * cols] + pltpu.roll(edges[hid:, i * cols : (i + 1) * cols], 1, 1)
            value = pltpu.roll(value, ahead, 1).astype(BF)

            @pl.when(fresh)
            def _(ref=ref, value=value):
                ref[:, half] = value

            @pl.when(jnp.logical_not(fresh))
            def _(ref=ref, value=value):
                ref[:, half] += value


def edge_maps(faces, rows, cols):
    maps = np.zeros((rows // 2, faces * cols, 2 * cols), np.float32)
    for rp in range(rows // 2):
        for f in range(faces):
            maps[rp, f * cols, f * rows + 2 * rp] = 1
            maps[rp, f * cols + cols - 1, cols + f * rows + 2 * rp] = 1
    return jnp.asarray(maps, BF)


def conv(x, top, bottom, left, right, weight, bias, last):
    face_count, rows, chans, cols = x.shape
    depth = weight.shape[1] // 4
    hid = weight.shape[0] // 2
    faces = 2
    scratch = [pltpu.VMEM((rows + 2, depth, faces * cols), BF)]
    if last:
        out_shape = jax.ShapeDtypeStruct((hid, face_count, rows, cols), BF)
        out_spec = pl.BlockSpec((hid, faces, rows, cols), lambda i: (0, i, 0, 0))
        scratch.append(pltpu.VMEM((faces, rows * (hid + 8), cols), F32))
    else:
        out_shape = [jax.ShapeDtypeStruct((face_count, rows, hid, cols), BF)]
        out_shape += [jax.ShapeDtypeStruct((hid, 2 * cols), BF)] * 2
        out_spec = [pl.BlockSpec((faces, rows, hid, cols), lambda i: (i, 0, 0, 0))]
        out_spec += [pl.BlockSpec((hid, 2 * cols), lambda i: (0, 0))] * 2
    return pl.pallas_call(
        functools.partial(conv_kernel, last=last),
        grid=(face_count // faces,),
        in_specs=[
            pl.BlockSpec(weight.shape, lambda i: (0, 0)),
            pl.BlockSpec(bias.shape, lambda i: (0, 0)),
            pl.BlockSpec((faces, rows, chans, cols), lambda i: (i, 0, 0, 0)),
            pl.BlockSpec((faces, chans, cols), lambda i: (i, 0, 0)),
            pl.BlockSpec((faces, chans, cols), lambda i: (i, 0, 0)),
            pl.BlockSpec(left.shape, lambda i: (0, 0)),
            pl.BlockSpec(right.shape, lambda i: (0, 0)),
        ]
        + ([] if last else [pl.BlockSpec((rows // 2, faces * cols, 2 * cols), lambda i: (0, 0, 0))]),
        out_specs=out_spec,
        out_shape=out_shape,
        scratch_shapes=scratch,
        compiler_params=pltpu.CompilerParams(vmem_limit_bytes=VMEM_LIMIT),
    )(weight, bias, x, top, bottom, left, right, *([] if last else [edge_maps(faces, rows, cols)]))


def wide_weight(weight, depth):
    taps, hid, chans = weight.shape
    rows = weight.reshape(3, 3, hid, chans).transpose(2, 0, 1, 3).reshape(hid, 3, 3 * chans)
    rows = jnp.pad(rows, ((0, 0), (0, 0), (0, depth - 3 * chans)))
    first = jnp.pad(rows, ((0, 0), (0, 1), (0, 0)))
    second = jnp.pad(rows, ((0, 0), (1, 0), (0, 0)))
    return jnp.stack([first, second]).reshape(2 * hid, 4 * depth)


class Plan:
    def __init__(self, bands, tiles):
        self.bands, self.tiles = bands, tiles
        self.per = bands // tiles
        per, last = self.per, bands - 1
        rounds = per + 1
        count = bands * tiles
        self.pairs = [[] for _ in range(rounds)]
        self.sends = np.zeros((rounds, count), np.int32)
        self.row_from = np.full((count, per), 2, np.int32)
        self.col_round = np.full((count,), rounds, np.int32)
        near, far = 0, last * tiles + tiles - 1
        corners = (tiles - 1, last * tiles)
        self.pairs[0].append((near, corners[1]))
        self.pairs[per - 1].append((far, corners[0]))
        self.pairs[per] = [(near, corners[0]), (far, corners[1])]
        self.sends[per, near], self.sends[per, far] = 1, 2

        def join(row_dev, col_dev, j):
            if row_dev in corners and col_dev in corners:
                self.row_from[row_dev, j] = 0
                self.col_round[col_dev] = per
            elif row_dev != col_dev:
                self.sends[j, row_dev] = 1
                self.pairs[j] += [(row_dev, col_dev), (col_dev, row_dev)]
                self.row_from[row_dev, j] = 0
                self.col_round[col_dev] = j

        for j in range(per):
            for t in range(tiles):
                join(t, (per * t + j) * tiles, j)
                join(last * tiles + t, (per * t + j) * tiles + tiles - 1, j)
        for pairs in self.pairs:
            assert len({a for a, _ in pairs}) == len(pairs) == len({b for _, b in pairs})
        self.flip_row = [
            (b * tiles + t, b * tiles + tiles - 1 - t) for b in (0, last) for t in range(tiles)
        ]
        self.flip_col = [(b * tiles + t, (last - b) * tiles + t) for b in range(bands) for t in (0, tiles - 1)]


def lane18(f, p, span, width):
    return (f // 6) * width + (f % 6) * span + p


def fixed_maps(faces, rows, cols):
    span = rows + 2
    own = np.zeros((3 * cols, 2 * cols), np.float32)
    wrap = np.zeros((4 * cols, 2 * cols), np.float32)
    widen = np.zeros((2 * cols, 2 * cols), np.float32)
    ends = np.zeros((2, 2 * cols, 2 * cols), np.float32)
    corner = np.zeros((2, 4 * cols, cols), np.float32)
    unit_ends = np.zeros((2, 2 * cols, 4 * cols), np.float32)
    for f in range(faces):
        for r in range(rows):
            to = lane18(f, r + 1, span, cols)
            own[f * rows + r, to] = wrap[f * rows + r, to] = widen[f * rows + r, to] = 1
        for which, p in ((0, 0), (1, span - 1)):
            to = lane18(f, p, span, cols)
            own[2 * cols + 16 * which + f, to] = 1
            wrap[(2 + which) * cols + 2 * f, to] = 1
            for side in range(2):
                ends[side, which * cols + 2 * f + side, to] = 1
        for which, r in ((0, 0), (1, rows - 1)):
            for side in range(2):
                corner[which, side * 2 * cols + f * rows + r, 2 * f + side] = 1
        for which, p in ((0, 0), (1, span - 1)):
            for pair in range(2):
                to = pair * 2 * cols + lane18(f, p, span, cols)
                unit_ends[which, pair * cols + 2 * f + which, to] = 1
    back = np.eye(cols)[::-1].copy()
    return [jnp.asarray(m, BF) for m in (own, wrap, widen, ends, corner, unit_ends, back)]


def seam_tables(seam_table, plan, rows, cols):
    band, tile = lax.axis_index("band"), lax.axis_index("tile")
    me = band * plan.tiles + tile
    faces = seam_table.shape[0]
    span = rows + 2
    per, rounds = plan.per, plan.per + 1
    last_band, last_tile = plan.bands - 1, plan.tiles - 1
    static = np.concatenate(
        [
            plan.col_round[:, None],
            plan.row_from[:, :1],
            plan.row_from[:, -1:],
            plan.sends.T,
        ],
        axis=1,
    ).astype(np.int32)
    static = lax.dynamic_slice_in_dim(jnp.asarray(static), me, 1, 0)[0]
    row = jnp.where(band == 0, seam_table[:, 0], seam_table[:, 1])
    col = jnp.where(tile == 0, seam_table[:, 2], seam_table[:, 3])
    scalars = jnp.concatenate(
        [jnp.stack([band, tile]).astype(jnp.int32), static, row[:, 1], row[:, 0], row[:, 2], jnp.zeros((4,), jnp.int32)]
    )
    lanes = np.full((2, 2 * cols), -1, np.int32)
    for f in range(faces):
        for p in range(span):
            lanes[:, lane18(f, p, span, cols)] = f, p
    face, place = lanes
    line_in = np.concatenate([np.where(face >= 0, face + faces * side, -1) for side in range(4)])
    place_in = np.tile(place, 4)
    col_line = col[:, 1] * faces + col[:, 0]
    hot = jnp.asarray(face[:, None] == np.arange(faces)[None, :])
    want = jnp.sum(jnp.where(hot, col_line[None, :], 0), axis=1)
    turned = jnp.sum(jnp.where(hot, col[:, 2][None, :], 0), axis=1)
    pick = (jnp.asarray(line_in)[:, None] == want[None, :]) & jnp.asarray(
        (place_in[:, None] == place[None, :]) & (face >= 0)[None, :]
    )
    corner = ((band == 0) & jnp.asarray(place == 0)) | ((band == last_band) & jnp.asarray(place == span - 1))
    same_face = (face[:, None] == face[None, :]) & (face >= 0)[None, :]
    keep = jnp.asarray(same_face & (place[:, None] == place[None, :])) & (turned == 0)[None, :]
    flip = jnp.asarray(same_face & (place[:, None] == span - 1 - place[None, :])) & (turned == 1)[None, :]
    join = jnp.concatenate([keep, flip]) & jnp.logical_not(corner)[None, :]
    at = np.arange(cols)
    end_face, end_side = np.where(at < 2 * faces, at // 2, -1), at % 2
    end_turned = jnp.sum(jnp.where(jnp.asarray(end_face[:, None] == np.arange(faces)[None, :]), row[:, 2][None, :], 0), axis=1)
    outer = ((tile == 0) & jnp.asarray(end_side == 0)) | ((tile == last_tile) & jnp.asarray(end_side == 1))
    same_end = (end_face[:, None] == end_face[None, :]) & (end_face >= 0)[None, :]
    keep_end = jnp.asarray(same_end & (end_side[:, None] == end_side[None, :])) & (end_turned == 0)[None, :]
    flip_end = jnp.asarray(same_end & (end_side[:, None] != end_side[None, :])) & (end_turned == 1)[None, :]
    join_end = jnp.concatenate([keep_end, flip_end]) & jnp.logical_not(outer)[None, :]
    return scalars, pick.astype(BF), join.astype(BF), join_end.astype(BF), fixed_maps(faces, rows, cols)


BAND, TILE, COL_ROUND, FIRST_FROM, LAST_FROM, SENDS = 0, 1, 2, 3, 4, 5


def whole(kernel, out_shape, scratch, scalars, *args):
    return pl.pallas_call(
        kernel,
        in_specs=[pl.BlockSpec(memory_space=pltpu.SMEM)] + [pl.BlockSpec(memory_space=pltpu.VMEM)] * len(args),
        out_specs=[pl.BlockSpec(memory_space=pltpu.VMEM)] * len(out_shape),
        out_shape=[jax.ShapeDtypeStruct(s, BF) for s in out_shape],
        scratch_shapes=scratch,
        compiler_params=pltpu.CompilerParams(vmem_limit_bytes=VMEM_LIMIT),
    )(scalars, *args)


def pick2(cond, a, b):
    return lax.select_n(cond, b, a)


def side_by_side(*parts):
    return jnp.concatenate(parts, axis=1)


def move(x, matrix):
    return jnp.dot(x, matrix, preferred_element_type=F32)


def rows_kernel(first_ref, last_ref, left_ref, right_ref, corner_ref, up_ref, down_ref):
    faces = first_ref.shape[0]
    both = side_by_side(left_ref[...], right_ref[...])
    for which, (src, out) in enumerate(((first_ref, up_ref), (last_ref, down_ref))):
        for f in range(faces):
            out[f] = src[f, 0]
        out[faces] = move(both, corner_ref[which]).astype(BF)


def rows_call(x, left, right, corner):
    faces, rows, chans, cols = x.shape
    full = lambda a: pl.BlockSpec(a.shape, lambda i: (0,) * a.ndim)
    out = jax.ShapeDtypeStruct((faces + 1, chans, cols), BF)
    return pl.pallas_call(
        rows_kernel,
        grid=(1,),
        in_specs=[
            pl.BlockSpec((faces, 1, chans, cols), lambda i: (0, 0, 0, 0)),
            pl.BlockSpec((faces, 1, chans, cols), lambda i: (0, rows - 1, 0, 0)),
            full(left),
            full(right),
            full(corner),
        ],
        out_specs=[pl.BlockSpec(out.shape, lambda i: (0, 0, 0))] * 2,
        out_shape=[out] * 2,
        compiler_params=pltpu.CompilerParams(vmem_limit_bytes=VMEM_LIMIT),
    )(x, x, left, right, corner)


def lines_kernel(s_ref, up_ref, down_ref, top_ref, bot_ref, low_ref, high_ref, left_ref, right_ref, own_ref, wrap_ref, ue_ref, *outs, bands, rows):
    messages, extra_ref, cl_ref = outs[:-2], outs[-2], outs[-1]
    per = len(messages)
    faces, (chans, cols) = up_ref.shape[0] - 1, up_ref.shape[1:]
    span = rows + 2
    kind = F32 if chans % 16 else BF
    first_band, first_tile = s_ref[BAND] == 0, s_ref[TILE] == 0
    lane = lax.broadcasted_iota(jnp.int32, (chans, cols), 1)
    top_edge = jnp.zeros((chans, cols), F32)
    for which, ref in enumerate((top_ref, bot_ref)):
        for f in range(faces):
            at = 16 * which + f
            row = ref[f].astype(F32)
            value = pltpu.roll(row, pick2(first_tile, jnp.int32(at), jnp.int32(at + 1)), 1)
            top_edge = jnp.where(lane == at, value, top_edge)
    mine = pick2(first_tile, low_ref[...], high_ref[...])
    theirs = pick2(first_tile, left_ref[...], right_ref[...])
    turn = pick2(first_tile, jnp.int32(0), jnp.int32(cols - 1))
    tc = pltpu.roll(top_ref[faces].astype(F32), turn, 1).astype(BF)
    bc = pltpu.roll(bot_ref[faces].astype(F32), turn, 1).astype(BF)
    own = move(side_by_side(mine, top_edge.astype(BF)), own_ref[...]).astype(BF)
    wrap = move(side_by_side(theirs, tc, bc), wrap_ref[...]).astype(BF)
    cl_ref[...] = side_by_side(pick2(first_tile, own, wrap), pick2(first_tile, wrap, own))
    on_row = jnp.logical_or(first_band, s_ref[BAND] == bands - 1)
    extra_ref[...] = jnp.zeros_like(extra_ref)
    for m in range(per):

        @pl.when(s_ref[SENDS + m] == 0)
        def _(m=m):
            messages[m][...] = cl_ref[...]

    @pl.when(on_row)
    def _():
        ends = side_by_side(pick2(first_band, up_ref[faces], bot_ref[faces]), pick2(first_band, top_ref[faces], down_ref[faces]))
        for g in range(4):
            pieces = [jnp.zeros((chans, cols), kind) for _ in range(per)]
            for i in range(6):
                pair, f = divmod(6 * g + i, faces)
                line = pick2(first_band, up_ref[f], bot_ref[f]) if pair == 0 else pick2(first_band, top_ref[f], down_ref[f])
                line = line.astype(kind)
                for j in range(per):
                    low = i * span + (1 if j == 0 else 0)
                    high = i * span + span - (1 if j == per - 1 else 0)
                    value = pltpu.roll(line, (i * span + 1 - rows * j) % cols, 1)
                    pieces[j] = jnp.where((lane >= low) & (lane < high), value, pieces[j])
            where = slice(g * cols, (g + 1) * cols)
            for j in (0, per - 1):
                pieces[j] = pieces[j] + move(ends, ue_ref[0 if j == 0 else 1, :, where]).astype(kind)
            for j in range(per):

                @pl.when(s_ref[SENDS + j] == 1)
                def _(j=j, piece=pieces[j]):
                    messages[j][:, where] = piece.astype(BF)

            for code, j in ((1, 0), (2, per - 1)):

                @pl.when(s_ref[SENDS + per] == code)
                def _(piece=pieces[j]):
                    extra_ref[:, where] = piece.astype(BF)


def seams_kernel(s_ref, *refs, rounds, rows, bands):
    got, refs = refs[:rounds], refs[rounds:]
    extra_ref, cl_ref, up_ref, down_ref, top_ref, bot_ref, pick_ref, srow_ref, scol_ref = refs[:9]
    rows_ref, unit0_ref, unit7_ref, other_ref, corner_ref = refs[9:]
    faces, (chans, cols) = up_ref.shape[0] - 1, up_ref.shape[1:]
    per = rounds - 1
    span = rows + 2
    first_band = s_ref[BAND] == 0
    kind = F32 if chans % 16 else BF
    lane = lax.broadcasted_iota(jnp.int32, (chans, cols), 1)
    for r in range(rounds):

        @pl.when(s_ref[COL_ROUND] == r)
        def _(r=r):
            other_ref[...] = got[r][...]

    @pl.when(s_ref[COL_ROUND] == rounds)
    def _():
        other_ref[...] = extra_ref[...]

    scol_ref[...] = move(side_by_side(other_ref[...], cl_ref[...]), pick_ref[...]).astype(BF)

    on_row = jnp.logical_or(first_band, s_ref[BAND] == bands - 1)
    table = SENDS + rounds

    @pl.when(on_row)
    def _():
        for code, to, normal in ((FIRST_FROM, unit0_ref, got[0]), (LAST_FROM, unit7_ref, got[per - 1])):
            for value, src in ((0, normal), (2, cl_ref)):

                @pl.when(s_ref[code] == value)
                def _(to=to, src=src):
                    to[...] = src[...]

        for f in range(faces + 1):
            rows_ref[f] = pick2(first_band, up_ref[f], bot_ref[f])
            rows_ref[faces + 1 + f] = pick2(first_band, top_ref[f], down_ref[f])
        units = [unit0_ref, *got[1 : per - 1], unit7_ref]
        corner_ref[...] = jnp.zeros_like(corner_ref)
        for f in range(faces):
            side, face = s_ref[table + f], s_ref[table + faces + f]

            @pl.when(side < 2)
            def _(f=f, side=side, face=face):
                srow_ref[f] = rows_ref[side * (faces + 1) + face]
                ends = rows_ref[side * (faces + 1) + faces].astype(F32)
                ends = pltpu.roll(ends, lax.rem(2 * f + 2 * cols - 2 * face, cols), 1)
                corner_ref[...] = jnp.where((lane == 2 * f) | (lane == 2 * f + 1), ends, corner_ref[...])

            @pl.when(side >= 2)
            def _(f=f, side=side, face=face):
                group = pl.ds(pl.multiple_of(((side - 2) * 2 + face // 6) * cols, cols), cols)
                q = lax.rem(face, 6) * span
                line = jnp.zeros((chans, cols), kind)
                ends = corner_ref[...]
                for j in range(per):
                    value = units[j][:, group].astype(kind)
                    line = jnp.where(lane // rows == j, pltpu.roll(value, lax.rem(rows * j + 2 * cols - 1 - q, cols), 1), line)
                    if j == 0:
                        ends = jnp.where(lane == 2 * f, pltpu.roll(value.astype(F32), lax.rem(2 * f + 2 * cols - q, cols), 1), ends)
                    if j == per - 1:
                        shift = lax.rem(2 * f + 1 + 2 * cols - q - (span - 1), cols)
                        ends = jnp.where(lane == 2 * f + 1, pltpu.roll(value.astype(F32), shift, 1), ends)
                srow_ref[f] = line.astype(BF)
                corner_ref[...] = ends

        srow_ref[faces] = corner_ref[...].astype(BF)

    @pl.when(jnp.logical_not(on_row))
    def _():
        srow_ref[...] = jnp.zeros_like(srow_ref)


def halo_kernel(s_ref, srow_ref, rrow_ref, scol_ref, rcol_ref, top_ref, bot_ref, left_ref, right_ref, join_ref, joinend_ref, back_ref, widen_ref, ends_ref, t_out, b_out, l_out, r_out, *, bands, tiles, rounds):
    faces, (chans, cols) = top_ref.shape[0] - 1, top_ref.shape[1:]
    first_band, last_band = s_ref[BAND] == 0, s_ref[BAND] == bands - 1
    first_tile, last_tile = s_ref[TILE] == 0, s_ref[TILE] == tiles - 1
    table = SENDS + rounds + 2 * faces
    for cond, out, ref in ((first_band, t_out, top_ref), (last_band, b_out, bot_ref)):

        @pl.when(cond)
        def _(out=out):
            for f in range(faces):
                turned = move(rrow_ref[f], back_ref[...]).astype(BF)
                out[f] = pick2(s_ref[table + f] == 1, turned, srow_ref[f])

        @pl.when(jnp.logical_not(cond))
        def _(out=out, ref=ref):
            for f in range(faces):
                out[f] = ref[f]

    ends = move(side_by_side(srow_ref[faces], rrow_ref[faces]), joinend_ref[...]).astype(BF)
    top_end = pick2(first_band, ends, top_ref[faces])
    bot_end = pick2(last_band, ends, bot_ref[faces])
    none = jnp.zeros_like(top_end)
    seam = move(side_by_side(scol_ref[...], rcol_ref[...]), join_ref[...])
    for side, (at_edge, src, out) in enumerate(((first_tile, left_ref, l_out), (last_tile, right_ref, r_out))):
        use_top = jnp.logical_or(first_band, jnp.logical_not(at_edge))
        use_bot = jnp.logical_or(last_band, jnp.logical_not(at_edge))
        both = side_by_side(pick2(use_top, top_end, none), pick2(use_bot, bot_end, none))
        base = pick2(at_edge, seam, move(src[...], widen_ref[...]))
        out[...] = (base + move(both, ends_ref[side])).astype(BF)


def exchange(x, low, high, plan, tables):
    scalars, pick, join, join_end, (own, wrap, widen, ends, corner, unit_ends, back) = tables
    faces, rows, chans, cols = x.shape
    bands, tiles = plan.bands, plan.tiles
    rounds = len(plan.pairs)
    across = [(i, (i + 1) % tiles) for i in range(tiles)]
    left = lax.ppermute(high, "tile", across)
    right = lax.ppermute(low, "tile", [(j, i) for i, j in across])
    up, down = rows_call(x, left, right, corner)
    around = [(i, (i + 1) % bands) for i in range(bands)]
    top = lax.ppermute(down, "band", around)
    bottom = lax.ppermute(up, "band", [(j, i) for i, j in around])
    outs = whole(
        functools.partial(lines_kernel, bands=bands, rows=rows),
        [(chans, 4 * cols)] * plan.per + [(chans, 4 * cols)] * 2,
        [],
        scalars, up, down, top, bottom, low, high, left, right, own, wrap, unit_ends,
    )
    messages, col_lines = outs[:-1], outs[-1]
    got = [lax.ppermute(m, AXES, pairs) for m, pairs in zip(messages, plan.pairs)]
    line = (faces + 1, chans, cols)
    srow, scol = whole(
        functools.partial(seams_kernel, rounds=rounds, rows=rows, bands=bands),
        [line, (chans, 2 * cols)],
        [
            pltpu.VMEM((2 * (faces + 1), chans, cols), BF),
            pltpu.VMEM((chans, 4 * cols), BF),
            pltpu.VMEM((chans, 4 * cols), BF),
            pltpu.VMEM((chans, 4 * cols), BF),
            pltpu.VMEM((chans, cols), F32),
        ],
        scalars, *got, messages[-1], col_lines, up, down, top, bottom, pick,
    )
    rrow = lax.ppermute(srow, AXES, plan.flip_row)
    rcol = lax.ppermute(scol, AXES, plan.flip_col)
    rim = (faces, chans, cols)
    return whole(
        functools.partial(halo_kernel, bands=bands, tiles=tiles, rounds=rounds),
        [rim, rim, (chans, 2 * cols), (chans, 2 * cols)],
        [],
        scalars, srow, rrow, scol, rcol, top, bottom, left, right, join, join_end, back, widen, ends,
    )


def local(
    source,
    regrid_weights,
    dest_group,
    dest_block,
    seam_table,
    conv1_weight,
    conv1_bias,
    conv2_weight,
    conv2_bias,
):
    bands, tiles = lax.axis_size("band"), lax.axis_size("tile")
    devices = bands * tiles
    src_count, top_count, block_len = regrid_weights.shape[:3]
    capacity = 3 * src_count * top_count // devices
    rows = block_len * tiles // bands
    faces = seam_table.shape[0]
    slots_dev = faces * rows
    fields = source.shape[0]
    hid = conv1_weight.shape[1]
    items = src_count * top_count
    total = devices * capacity

    target = dest_group.reshape(items)
    order = jnp.arange(items)
    same = (target[:, None] == target[None, :]) & (order[None, :] < order[:, None])
    rank = jnp.sum(same.astype(jnp.int32), axis=1)
    position = target * capacity + rank
    hit = position[:, None] == jnp.arange(total)[None, :]
    out_slots = slots_dev + jnp.sum(
        jnp.where(hit, (dest_block.reshape(items) - slots_dev)[:, None], 0), axis=0
    )
    out_slots = jnp.pad(
        out_slots.reshape(devices, 1, capacity).astype(BF), ((0, 0), (0, 7), (0, block_len - capacity))
    )
    outgoing = regrid(
        source, regrid_weights, jnp.concatenate([target, rank * (fields // 8)]), out_slots, capacity
    )
    arrived = lax.all_to_all(outgoing, AXES, split_axis=0, concat_axis=0, tiled=True)
    slots = arrived[:, -1, 0, :capacity].astype(jnp.int32).reshape(total)
    regridded, low, high = place(arrived, slots, slots_dev)
    regridded = regridded.reshape(faces, rows, fields, block_len)

    plan = Plan(bands, tiles)
    tables = seam_tables(seam_table, plan, rows, block_len)
    depth1 = -(-3 * fields // 128) * 128
    weight1 = wide_weight(conv1_weight, depth1)
    weight2 = wide_weight(conv2_weight, 3 * hid)
    bias1 = jnp.concatenate([conv1_bias, conv1_bias])[:, None]
    bias2 = jnp.concatenate([conv2_bias, conv2_bias])[:, None]
    halo = exchange(regridded, low, high, plan, tables)
    hidden, low, high = conv(regridded, *halo, weight1, bias1, False)
    halo = exchange(hidden, low, high, plan, tables)
    return conv(hidden, *halo, weight2, bias2, True)


def solution(mesh):
    return jax.shard_map(
        local,
        mesh=mesh,
        in_specs=(
            P(None, AXES),
            P(AXES, None, None, None),
            P(AXES, None),
            P(AXES, None),
            P(),
            P(),
            P(),
            P(),
            P(),
        ),
        out_specs=P(None, None, "band", "tile"),
        check_vma=False,
    )
```
